128 devices in a mesh: grp: 4 (over z_lo, core), dev: 32 (over y, z_hi, x).
Axes of the slice: x: 4, y: 4, z: 4 (z_hi: 2, z_lo: 2; z = z_hi * 2 + z_lo), core: 2. Of those that a mesh axis runs over, the one named last changes fastest.
Arguments:
- span_q: bfloat16 [1536, 4096], P('grp', 'dev'), may hold values from -8 to 8, as said below
- span_kv: bfloat16 [12, 1024, 128], P('grp', None, 'dev'), may hold values from -6 to 6
- kv_cache: bfloat16 [12, 1024, 8192], P('grp', None, 'dev'), may hold values from -4.5 to 4.5
- resid: bfloat16 [1536, 4096], P('grp', 'dev')
- o_weight: bfloat16 [4096, 4096], P('dev'), may hold values from -0.1875 to 0.1875
- norm_gain: float32 [4096], P('dev'), may hold values from 0.1 to 1.9
- w_gate: bfloat16 [4096, 16384], P(None, 'dev'), may hold values from -0.09375 to 0.09375
- w_up: bfloat16 [4096, 16384], P(None, 'dev'), may hold values from -0.09375 to 0.09375
- w_down: bfloat16 [16384, 4096], P('dev'), may hold values from -0.09375 to 0.09375
- cached_len: int32 [12], P('grp'), may hold values from 2 to 8192, as said below
- page_table: int32 [396], P('grp'), may hold values from 0 to 395, each once
Outputs:
- layer_out: bfloat16 [1536, 4096], P('grp', 'dev')
- decode_pool: bfloat16 [396, 1024, 256], P('grp', 'dev')
The draws below stay inside these ranges and needn't reach their ends.
Inputs may be any that keep to these rules, and one draw needn't show every extreme that they name: `span_q`: query values; the hidden draw holds some rows far larger. `cached_len`: some group has exactly 8192 cached positions in every draw. `page_table`: every slot is named exactly once.
All inputs are finite; a program needn't handle non-finite values.
Results may differ from the reference program's by a relative error of at most 0.017.
Values may be sent and summed in bfloat16 or wider, within the bound.
A program may use at most 128 MiB of HBM per device.

```python
import jax
import jax.numpy as jnp
from jax import lax

D = 4096
HQ = 32
KVH = 4
HD = 128
FF = 16384
SPAN = 128
PAGE = 256
G = 12
TOKENS = 1536
S_MAX = 8192
NB = 33
SLOTS = 396
KVW = 1024


def draw_span_q(key, part):
    inner = jax.random.fold_in(key, 11)
    value = jnp.clip(jax.random.normal(inner, (TOKENS, HQ * HD), jnp.float32), -4.5, 4.5)
    return value.astype(jnp.bfloat16)


def draw_kv_cache(key, part):
    inner = jax.random.fold_in(key, 12)
    value = jnp.clip(jax.random.normal(inner, (G, KVW, S_MAX), jnp.float32), -4.5, 4.5)
    return value.astype(jnp.bfloat16)


def draw_resid(key, part):
    inner = jax.random.fold_in(key, 13)
    column = jnp.arange(D).astype(jnp.float32) / (D - 1)
    base = jnp.clip(jax.random.normal(inner, (TOKENS, D), jnp.float32), -4.5, 4.5)
    value = base * (0.6 + 1.2 * column)[None, :]
    return value.astype(jnp.bfloat16)


def draw_cached_len(key, part):
    lengths = jax.random.randint(jax.random.fold_in(key, 14), (G,), 2, S_MAX + 1, jnp.int32)
    longest = jax.random.randint(jax.random.fold_in(key, 15), (), 0, G, jnp.int32)
    return jnp.where(jnp.arange(G) == longest, S_MAX, lengths).astype(jnp.int32)


def with_spikes(entries, rng, source, target, shards_of, factor):
    owner, partner = [(jnp.arange(entries.shape[axis_at]) // (entries.shape[axis_at] // shards_of)).reshape([-1 if axis == axis_at else 1 for axis in range(entries.ndim)]) for axis_at in (source, target)]
    chosen = jax.random.permutation(rng, shards_of)[partner]
    strong = (owner == chosen) | (owner == (partner + shards_of // 2) % shards_of)
    return jnp.where(strong, factor * entries, entries)


def steps_of(rng, dims, split, smallest, largest):
    def one(dim, blocks):
        draws = jax.random.uniform(jax.random.fold_in(jax.random.fold_in(rng, 6), dim), (blocks,), jnp.float32, smallest / len(split), largest / len(split))
        return jnp.repeat(jnp.exp(draws), dims[dim] // blocks).reshape((-1,) + (1,) * (len(dims) - dim - 1))

    factor_of = one(*split[0])
    for cut in split[1:]:
        factor_of = factor_of * one(*cut)
    return factor_of


def bell_draw(key, shape, spread, reach, shards=(), kind=jnp.bfloat16):
    values = spread * jax.random.normal(key, shape, jnp.float32)
    if shards:
        values = values * steps_of(key, shape, shards, -0.22, 0.18)
    return jnp.clip(values, -reach, reach).astype(kind)


def heavy_noise(own_key, dims, deviation, bound, split, heavy, held_as=jnp.bfloat16):
    drawn = deviation * jax.random.normal(own_key, dims, jnp.float32)
    if split:
        drawn = drawn * steps_of(own_key, dims, split, -0.22, 0.18)
    return jnp.clip(with_spikes(drawn, jax.random.fold_in(own_key, 3), *heavy), -bound, bound).astype(held_as)


def setup_inputs(seed: int = 0) -> dict:
    arg_keys = jax.random.split(jax.random.key(seed), 12)
    span_q = draw_span_q(jax.random.fold_in(arg_keys[11], 71), 0)
    span_kv = bell_draw(arg_keys[1], (G, KVW, SPAN), 1.0, 6.0, ((0, 4), (2, 32)))
    kv_cache = draw_kv_cache(jax.random.fold_in(arg_keys[11], 71), 0)
    resid = draw_resid(jax.random.fold_in(arg_keys[11], 71), 0)
    o_weight = heavy_noise(arg_keys[4], (HQ * HD, D), (HQ * HD) ** -0.5, 0.1875, ((0, 32),), (0, 1, 32, 2.75))
    norm_gain = jnp.clip(1.0 + 0.18 * jax.random.normal(arg_keys[5], (D,), jnp.float32), 0.1, 1.9)
    w_gate = bell_draw(arg_keys[6], (D, FF), D ** -0.5, 0.09375, ((1, 32),))
    w_up = bell_draw(arg_keys[7], (D, FF), D ** -0.5, 0.09375, ((1, 32),))
    w_down = heavy_noise(arg_keys[8], (FF, D), FF ** -0.5, 0.09375, ((0, 32),), (0, 1, 32, 2.75))
    cached_len = draw_cached_len(jax.random.fold_in(arg_keys[11], 71), 0)
    page_table = jax.random.permutation(arg_keys[10], SLOTS).astype(jnp.int32)
    return {"span_q": span_q, "span_kv": span_kv, "kv_cache": kv_cache, "resid": resid, "o_weight": o_weight, "norm_gain": norm_gain, "w_gate": w_gate, "w_up": w_up, "w_down": w_down, "cached_len": cached_len, "page_table": page_table}


def attend_group(items):
    q_rows, span_g, cache_g, length = items
    grouped = HQ // KVH
    queries = q_rows.reshape(SPAN, KVH, grouped, HD).transpose(1, 0, 2, 3).reshape(KVH, SPAN * grouped, HD)
    cache_h = cache_g.reshape(KVH, 2, HD, S_MAX)
    span_h = span_g.reshape(KVH, 2, HD, SPAN)
    token = jnp.arange(SPAN * grouped) // grouped
    cache_ok = jnp.broadcast_to((jnp.arange(S_MAX) < length)[None, :], (SPAN * grouped, S_MAX))
    span_ok = jnp.arange(SPAN)[None, :] <= token[:, None]
    valid = jnp.concatenate([cache_ok, span_ok], axis=1)

    def one_head(parts):
        query, cached, fresh = parts
        keys = jnp.concatenate([cached[0], fresh[0]], axis=1)
        values = jnp.concatenate([cached[1], fresh[1]], axis=1)
        score = jnp.dot(query, keys, preferred_element_type=jnp.float32) * (1.0 / HD ** 0.5)
        highest = lax.optimization_barrier(jnp.max(jnp.where(valid, score, -1e+30), axis=1, keepdims=True))
        weight = jnp.where(valid, jnp.exp(score - highest), 0.0)
        total = lax.optimization_barrier(jnp.sum(weight, axis=1))
        summed = lax.dot_general(weight.astype(jnp.bfloat16), values, (((1,), (1,)), ((), ())), preferred_element_type=jnp.float32)
        return (summed / total[:, None]).astype(jnp.bfloat16)
    result = lax.map(one_head, (queries, cache_h, span_h))
    return result.reshape(KVH, SPAN, grouped, HD).transpose(1, 0, 2, 3).reshape(SPAN, HQ * HD)

def build_pages(items):
    cache_g, span_g, length = items
    position = jnp.arange(S_MAX)
    kept = jnp.where(position[None, :] < length, cache_g, 0.0)
    filler = jnp.zeros((KVW, NB * PAGE - S_MAX), kept.dtype)
    prefix = jnp.concatenate([kept, filler], axis=1)
    prefix = lax.dynamic_update_slice(prefix, span_g, (jnp.int32(0), length.astype(jnp.int32)))
    return prefix.reshape(KVW, NB, PAGE).transpose(1, 0, 2)

def reference(span_q, span_kv, kv_cache, resid, o_weight, norm_gain, w_gate, w_up, w_down, cached_len, page_table):
    attn = lax.map(attend_group, (span_q.reshape(G, SPAN, HQ * HD), span_kv, kv_cache, cached_len))
    attn = attn.reshape(TOKENS, HQ * HD)
    proj = jnp.dot(attn, o_weight, preferred_element_type=jnp.float32)
    h_mid = (resid.astype(jnp.float32) + proj).astype(jnp.bfloat16)
    wide = h_mid.astype(jnp.float32)
    mean_sq = lax.optimization_barrier(jnp.mean(wide * wide, axis=1, keepdims=True))
    normed = (wide * lax.rsqrt(mean_sq + 1e-05) * norm_gain[None, :]).astype(jnp.bfloat16)
    gate = jnp.dot(normed, w_gate, preferred_element_type=jnp.float32)
    upward = jnp.dot(normed, w_up, preferred_element_type=jnp.float32)
    hidden = (jax.nn.silu(gate) * upward).astype(jnp.bfloat16)
    mlp = jnp.dot(hidden, w_down, preferred_element_type=jnp.float32)
    layer_out = (h_mid.astype(jnp.float32) + mlp).astype(jnp.bfloat16)
    pages = lax.map(build_pages, (kv_cache, span_kv, cached_len)).reshape(SLOTS, KVW, PAGE)
    decode_pool = jnp.zeros((SLOTS, KVW, PAGE), pages.dtype).at[page_table].set(pages)
    return (layer_out, decode_pool)
```

```python
import functools

import jax
import jax.numpy as jnp
from jax import lax
from jax.experimental import pallas as pl
from jax.experimental.pallas import tpu as pltpu
from jax.sharding import PartitionSpec as P

D = 4096
HD = 128
KVH = 4
PAGE = 256
G_DEV = 3
NB = 33
SPAN = 128
NY = 4
NC = 8
TOK = 384
HALF = 192
FF_DEV = 512
NEG = -1e30
SCALE = 1.4426950408889634 / HD**0.5
BF = jnp.bfloat16
F32 = jnp.float32
MESH = pl.DeviceIdType.MESH


def mult(value, by):
    return pl.multiple_of(value, by)


def dot(a, b, dims=(((1,), (0,)), ((), ()))):
    return lax.dot_general(a, b, dims, preferred_element_type=F32)


def layer_kernel(
    q_ref, skv_ref, kv_hbm, resid_ref, ow_hbm, gain_ref, wg_hbm, wu_hbm, wd_hbm, len_ref,
    out_ref, ep, fs,
    ow, wg, wu, wd, kv, qt, qg, fr_src, fr, tr, ns, nr, att,
    sa1, ra1, sb1, rb1, ta1, tra1, tb1, trb1,
    sa2, ra2, sb2, rb2, ta2, tra2, tb2, trb2,
    xa, xb, hm, ss, st, hidden, acc_ref, fa, fb,
    w_sem, kv_loc, ep_loc,
    kv_s, kv_r, q_s, q_r, f_s, f_r, n_s, n_r,
    y_s, y_r, c_s, c_r, e_s, e_r, t_s, t_r, g_s, g_r, gt_s, gt_r,
):
    grp = lax.axis_index("grp")
    me = lax.axis_index("dev")
    y = me // NC
    c = lax.rem(me, NC)
    core = lax.rem(grp, 2)
    sibling = grp + 1 - 2 * core
    across = lax.rem(grp + 2, 4)

    def y_peer(k):
        return lax.rem(y + k, NY)

    def c_peer(j):
        return lax.rem(c + j, NC)

    def to_y(src, dst, send, recv, k):
        return pltpu.make_async_remote_copy(
            src_ref=src, dst_ref=dst, send_sem=send, recv_sem=recv,
            device_id=(grp, y_peer(k) * NC + c), device_id_type=MESH)

    def to_c(src, dst, send, recv, j):
        return pltpu.make_async_remote_copy(
            src_ref=src, dst_ref=dst, send_sem=send, recv_sem=recv,
            device_id=(grp, y * NC + c_peer(j)), device_id_type=MESH)

    def to_grp(src, dst, send, recv, target):
        return pltpu.make_async_remote_copy(
            src_ref=src, dst_ref=dst, send_sem=send, recv_sem=recv,
            device_id=(target, me), device_id_type=MESH)

    def loop_c(body):
        def step(j, carry):
            body(j)
            return carry

        lax.fori_loop(1, NC, step, 0)

    barrier = pltpu.get_barrier_semaphore()
    for k in range(1, NY):
        pl.semaphore_signal(barrier, inc=1, device_id=(grp, y_peer(k) * NC + c), device_id_type=MESH)
    loop_c(lambda j: pl.semaphore_signal(
        barrier, inc=1, device_id=(grp, y * NC + c_peer(j)), device_id_type=MESH))
    for other in (sibling, across):
        pl.semaphore_signal(barrier, inc=1, device_id=(other, me), device_id_type=MESH)

    own_kv = [
        pltpu.make_async_copy(
            kv_hbm.at[g, pl.ds(mult(y * 256, 256), 256)], kv.at[0, g], kv_loc.at[g]
        )
        for g in range(G_DEV)
    ]
    for copy in own_kv:
        copy.start()
    for g in range(G_DEV):
        qt[g] = q_ref[g * SPAN : (g + 1) * SPAN, :].astype(F32).T.astype(BF)
    fresh = jnp.zeros((16, 1024), F32)
    for g in range(G_DEV):
        row = lax.broadcasted_iota(jnp.int32, (16, 4), 0)
        col = lax.broadcasted_iota(jnp.int32, (16, 4), 1)
        pick = jnp.where(row == col + 4 * g, 1.0, 0.0).astype(BF)
        fresh = fresh + dot(pick, skv_ref[g], (((1,), (1,)), ((), ())))
    fr_src[...] = fresh.astype(BF)
    pl.semaphore_wait(barrier, NY - 1 + NC - 1 + 2)

    def q_copy(j):
        return to_c(qt, qg.at[:, :, pl.ds(mult(j * HD, HD), HD)], q_s.at[j], q_r.at[j], j)

    def f_copy(k):
        return to_y(
            fr_src.at[:, pl.ds(mult(y_peer(k) * 256, 256), 256)], fr.at[k], f_s.at[k], f_r.at[k], k
        )

    def kv_copy(k, g):
        return to_y(
            kv_hbm.at[g, pl.ds(mult(y_peer(k) * 256, 256), 256)],
            kv.at[k, g], kv_s.at[k, g], kv_r.at[k, g], k)

    loop_c(lambda j: q_copy(j).start())
    for k in range(1, NY):
        f_copy(k).start()
    for g in range(G_DEV):
        for k in (1, 3, 2):
            kv_copy(k, g).start()
    weights = [
        pltpu.make_async_copy(src, dst, w_sem.at[i])
        for i, (src, dst) in enumerate(((ow_hbm, ow), (wg_hbm, wg), (wu_hbm, wu), (wd_hbm, wd)))
    ]
    for copy in weights:
        copy.start()
    for g in range(G_DEV):
        qg[g, :, 0:HD] = qt[g]
    fr[0] = fr_src[:, pl.ds(mult(y * 256, 256), 256)]
    for k in range(1, NY):
        f_copy(k).wait_recv()
    fresh_rows = fr[...].reshape(64, 256)
    tr[...] = jnp.concatenate(
        [fresh_rows.astype(F32).T, jnp.zeros((256, 64), F32)], axis=1
    ).astype(BF)
    loop_c(lambda j: q_copy(j).wait_recv())

    rows = NC * SPAN
    top_dims = (((0,), (0,)), ((), ()))

    def n_copy(g, j):
        return to_c(ns.at[g, j], nr.at[g, j], n_s.at[g, j], n_r.at[g, j], j)

    for g in range(G_DEV):
        length = len_ref[g]
        high = jnp.full((1, rows), -1e20, F32)
        total = jnp.zeros((1, rows), F32)
        acc = jnp.zeros((HD, rows), F32)

        def block(score, value, high, total, acc):
            new = jnp.maximum(high, jnp.max(score, axis=0, keepdims=True))
            keep = jnp.exp2((high - new) * SCALE)
            weight = jnp.exp2((score - new) * SCALE)
            total = total * keep + jnp.sum(weight, axis=0, keepdims=True)
            acc = acc * keep + dot(value, weight.astype(BF))
            return new, total, acc

        r = lax.broadcasted_iota(jnp.int32, (64, rows), 0)
        token = lax.rem(lax.broadcasted_iota(jnp.int32, (64, rows), 1), SPAN)
        src_y = lax.rem(y - r // 16 + NY, NY)
        r16 = lax.rem(r, 16)
        fresh_at = (src_y * NC + c) * 4 + lax.rem(r16, 4)
        ok = (r16 // 4 == g) & (fresh_at <= token)
        score = dot(fresh_rows[:, 0:HD], qg[g])
        score = jnp.where(ok, score, NEG)
        high, total, acc = block(score, tr[HD : 2 * HD, 0:64], high, total, acc)
        for k in range(NY):
            if k == 0:
                own_kv[g].wait()
            else:
                kv_copy(k, g).wait_recv()
            first = (lax.rem(y - k + NY, NY) * NC + c) * PAGE
            at = first + lax.broadcasted_iota(jnp.int32, (PAGE, 1), 0)
            score = dot(kv[k, g, 0:HD, :], qg[g], top_dims)
            score = jnp.where(at < length, score, NEG)
            high, total, acc = block(score, kv[k, g, HD : 2 * HD, :], high, total, acc)
        some = total > 0.0
        scaled = acc * jnp.where(some, 1.0 / jnp.where(some, total, 1.0), 0.0)
        level = jnp.where(some, high * SCALE + jnp.log2(jnp.where(some, total, 1.0)), NEG)
        hi = level.astype(BF).astype(F32)
        mid = (level - hi).astype(BF).astype(F32)
        low = level - hi - mid
        which = lax.broadcasted_iota(jnp.int32, (16, rows), 0)
        tail = jnp.where(
            which == 0, hi, jnp.where(which == 1, mid, jnp.where(which == 2, low, 0.0))
        )
        for j in range(NC):
            lanes = slice(j * HD, (j + 1) * HD)
            dest = (NC - j) % NC
            buf = nr if dest == 0 else ns
            buf[g, dest, 0:HD, :] = scaled[:, lanes].astype(BF)
            buf[g, dest, HD : HD + 16, :] = tail[:, lanes].astype(BF)
        for j in range(1, NC):
            n_copy(g, j).start()

    def e_copy(j):
        return to_c(
            kv.at[:, :, pl.ds(mult(c_peer(j) * 32, 32), 32), :], ep.at[0, j], e_s.at[j], e_r.at[j], j
        )

    def t_copy(j):
        return to_c(
            tr.at[pl.ds(mult(c_peer(j) * 32, 32), 32), :], fs.at[0, j], t_s.at[j], t_r.at[j], j
        )

    for g in range(G_DEV):
        for j in range(1, NC):
            n_copy(g, j).wait_recv()
        levels = [
            jnp.sum(nr[g, j, HD : HD + 16, :].astype(F32), axis=0, keepdims=True) for j in range(NC)
        ]
        top = functools.reduce(jnp.maximum, levels)
        scales = [jnp.exp2(level - top) for level in levels]
        summed = sum(nr[g, j, 0:HD, :].astype(F32) * scales[j] for j in range(NC))
        att[g * SPAN : (g + 1) * SPAN, :] = (summed / sum(scales)).T.astype(BF)

    loop_c(lambda j: e_copy(j).start())
    loop_c(lambda j: t_copy(j).start())
    own_pages = [
        pltpu.make_async_copy(
            kv.at[:, :, pl.ds(mult(c * 32, 32), 32), :], ep.at[0, 0], ep_loc.at[0]
        ),
        pltpu.make_async_copy(tr.at[pl.ds(mult(c * 32, 32), 32), :], fs.at[0, 0], ep_loc.at[1]),
    ]
    for copy in own_pages:
        copy.start()

    def scatter(turn, lhs, w, sa, ra, sb, rb, ta, tra, tb, trb):
        def a1(k):
            return to_y(sa.at[k], ra.at[k], y_s.at[turn, k], y_r.at[turn, k], k)

        def b1(j):
            return to_c(sb.at[j], rb.at[j], c_s.at[turn, j], c_r.at[turn, j], j)

        def a2(j):
            return to_c(ta.at[j], tra.at[j], c_s.at[turn + 1, j], c_r.at[turn + 1, j], j)

        def b2(k):
            return to_y(tb.at[k], trb.at[k], y_s.at[turn + 1, k], y_r.at[turn + 1, k], k)

        def part_a(k):
            cols = pl.ds(mult(y_peer(k) * 1024, 1024), 1024)
            sa[k] = dot(lhs[0:HALF, :], w[:, cols]).astype(BF)

        def part_b(j):
            at = c_peer(j) * HD
            cols = jnp.concatenate(
                [w[:, pl.ds(mult(at + yy * 1024, HD), HD)] for yy in range(NY)], axis=1
            )
            sb[j] = dot(lhs[HALF:TOK, :], cols).astype(BF)

        def start_b(lo, hi):
            def step(j, carry):
                part_b(j)
                b1(j).start()
                return carry

            lax.fori_loop(lo, hi, step, 0)

        for k, (lo, hi) in ((1, (1, 3)), (3, (3, 5)), (2, (5, 8))):
            part_a(k)
            a1(k).start()
            start_b(lo, hi)
        part_a(0)
        part_b(0)
        for k in range(1, NY):
            a1(k).wait_recv()

        def sum_a(j):
            cols = pl.ds(mult(c_peer(j) * HD, HD), HD)
            value = sa[0, :, cols].astype(F32)
            for k in range(1, NY):
                value = value + ra[k, :, cols].astype(F32)
            return value

        def send_a(j):
            ta[j] = sum_a(j).astype(BF)
            a2(j).start()

        loop_c(send_a)
        fa[...] = sum_a(0)
        loop_c(lambda j: b1(j).wait_recv())

        def sum_b(k):
            cols = pl.ds(mult(y_peer(k) * HD, HD), HD)
            value = sb[0, :, cols].astype(F32)
            for j in range(1, NC):
                value = value + rb[j, :, cols].astype(F32)
            return value

        for k in range(1, NY):
            tb[k] = sum_b(k).astype(BF)
            b2(k).start()
        fb[...] = sum_b(0)
        for k in range(1, NY):
            b2(k).wait_recv()
            fb[...] += trb[k].astype(F32)

        def add_a(j):
            a2(j).wait_recv()
            fa[...] += tra[j].astype(F32)

        loop_c(add_a)

        def finish():
            for k in range(1, NY):
                a1(k).wait_send()
                b2(k).wait_send()

            def done(j):
                b1(j).wait_send()
                a2(j).wait_send()

            loop_c(done)

        return finish

    weights[0].wait()
    finish_1 = scatter(0, att, ow, sa1, ra1, sb1, rb1, ta1, tra1, tb1, trb1)

    my_cols = pl.ds(mult(c * HD, HD), HD)
    ones = jnp.ones((8, HD), F32)
    for half, (x, f) in enumerate(((xa, fa), (xb, fb))):
        span = slice(half * HALF, (half + 1) * HALF)
        mid_bf = (resid_ref[span, :].astype(F32) + f[...]).astype(BF)
        hm[span, :] = mid_bf
        wide = mid_bf.astype(F32)
        x[y, :, my_cols] = (wide * gain_ref[...]).astype(BF)
    wide = hm[...].astype(F32)
    ss[0] = lax.dot_general(
        ones, wide * wide, (((1,), (1,)), ((), ())),
        precision=lax.Precision.HIGHEST, preferred_element_type=F32)

    def xa1(j):
        view = xa.at[y, :, my_cols]
        return to_c(view, view, c_s.at[2, j], c_r.at[2, j], j)

    def xb1(k):
        view = xb.at[y, :, my_cols]
        return to_y(view, view, y_s.at[2, k], y_r.at[2, k], k)

    def xa2(k):
        return to_y(xa.at[y], xa.at[y], y_s.at[3, k], y_r.at[3, k], k)

    def xb2(j):
        view = xb.at[:, :, my_cols]
        return to_c(view, view, c_s.at[3, j], c_r.at[3, j], j)

    def ss1(j):
        return to_c(ss.at[0], ss.at[j], c_s.at[6, j], c_r.at[6, j], j)

    def st1(k):
        return to_y(st.at[0], st.at[k], y_s.at[6, k], y_r.at[6, k], k)

    for k in range(1, NY):
        xb1(k).start()
    loop_c(lambda j: xa1(j).start())
    loop_c(lambda j: ss1(j).start())
    for k in range(1, NY):
        xb1(k).wait_recv()
    loop_c(lambda j: xb2(j).start())
    loop_c(lambda j: xa1(j).wait_recv())
    for k in range(1, NY):
        xa2(k).start()
    loop_c(lambda j: ss1(j).wait_recv())
    st[0] = jnp.sum(ss[...], axis=0)
    for k in range(1, NY):
        st1(k).start()

    def g_copy(i):
        target = across if i == 2 else sibling
        from_slot = 2 if i == 3 else 0
        return (
            to_grp(ep.at[from_slot], ep.at[i], g_s.at[i], g_r.at[i], target),
            to_grp(fs.at[from_slot], fs.at[i], gt_s.at[i], gt_r.at[i], target),
        )

    for copy in own_pages:
        copy.wait()
    loop_c(lambda j: e_copy(j).wait_recv())
    loop_c(lambda j: t_copy(j).wait_recv())
    for i in (2, 1):
        for copy in g_copy(i):
            copy.start()

    weights[1].wait()
    weights[2].wait()
    for k in range(1, NY):
        st1(k).wait_recv()
    squares = jnp.sum(st[...], axis=0)
    factor = lax.rsqrt(squares * (1.0 / D) + 1e-5)
    factor = jnp.broadcast_to(factor[0:1, :], (HD, TOK)).T
    for k in range(1, NY):
        xa2(k).wait_recv()
    loop_c(lambda j: xb2(j).wait_recv())
    for half, x in enumerate((xa, xb)):
        span = slice(half * HALF, (half + 1) * HALF)
        scale = factor[span, 0:1]

        def tile(n, carry, x=x, span=span, scale=scale):
            cols = pl.ds(mult(n * 256, 256), 256)
            gate = jnp.zeros((HALF, 256), F32)
            upward = jnp.zeros((HALF, 256), F32)
            for yy in range(NY):
                deep = slice(yy * 1024, (yy + 1) * 1024)
                gate = gate + dot(x[yy], wg[deep, cols])
                upward = upward + dot(x[yy], wu[deep, cols])
            gate = gate * scale
            upward = upward * scale
            hidden[span, cols] = (gate / (1.0 + jnp.exp(-gate)) * upward).astype(BF)
            return carry

        lax.fori_loop(0, FF_DEV // 256, tile, 0)

    for copy in g_copy(2):
        copy.wait_recv()
    for copy in g_copy(3):
        copy.start()
    weights[3].wait()
    finish_2 = scatter(4, hidden, wd, sa2, ra2, sb2, rb2, ta2, tra2, tb2, trb2)
    out_ref[0:HALF, :] = (hm[0:HALF, :].astype(F32) + fa[...]).astype(BF)
    out_ref[HALF:TOK, :] = (hm[HALF:TOK, :].astype(F32) + fb[...]).astype(BF)

    for i in (1, 3):
        for copy in g_copy(i):
            copy.wait_recv()
    for i in (1, 2, 3):
        for copy in g_copy(i):
            copy.wait_send()
    finish_1()
    finish_2()
    for k in range(1, NY):
        f_copy(k).wait_send()
        xb1(k).wait_send()
        xa2(k).wait_send()
        st1(k).wait_send()
        for g in range(G_DEV):
            kv_copy(k, g).wait_send()

    def sent(j):
        q_copy(j).wait_send()
        e_copy(j).wait_send()
        t_copy(j).wait_send()
        xa1(j).wait_send()
        xb2(j).wait_send()
        ss1(j).wait_send()
        for g in range(G_DEV):
            n_copy(g, j).wait_send()

    loop_c(sent)


def page_kernel(ep, fs, table, lens, out_ref, rolled, inverse):
    grp = lax.axis_index("grp")
    me = lax.axis_index("dev")
    y = me // NC
    c = lax.rem(me, NC)
    pages = out_ref.shape[0]

    def put(n, carry):
        for i in range(6):
            inverse[table[n * 6 + i]] = n * 6 + i
        return carry

    lax.fori_loop(0, table.shape[0] // 6, put, 0)
    lane = lax.broadcasted_iota(jnp.int32, (HD, 1), 0)
    k = lane // 16
    r16 = lax.rem(lane, 16)
    column = lax.broadcasted_iota(jnp.int32, (HD, G_DEV * SPAN), 1)
    picks = []
    for j in range(NC):
        from_c = lax.rem(c - j + NC, NC)
        token = (lax.rem(y - k + 2 * NY, NY) * NC + from_c) * 4 + lax.rem(r16, 4)
        target = jnp.where((lane < 64) & (r16 < 12), (r16 // 4) * SPAN + token, -1)
        picks.append(jnp.where(column == target, 1.0, 0.0).astype(BF))
    for i in range(4):
        spans = sum(dot(fs[i, j], picks[j]) for j in range(NC))
        for g in range(G_DEV):
            length = lens[lax.bitwise_xor(grp, i) * G_DEV + g]
            padded = jnp.concatenate(
                [spans[:, g * SPAN : (g + 1) * SPAN], jnp.zeros((32, SPAN), F32)], axis=1
            )
            rolled[i * G_DEV + g] = pltpu.roll(padded, lax.rem(length, PAGE), 1)

    lanes = lax.broadcasted_iota(jnp.int32, (1, PAGE), 1)

    def page(s, carry):
        n = inverse[grp * pages + s]
        group = n // NB
        b = n - group * NB
        q = group // G_DEV
        g = group - q * G_DEV
        i = lax.bitwise_xor(grp, q)
        bb = jnp.minimum(b, 31)
        j = lax.bitwise_and(c - bb + 32, NC - 1)
        kk = lax.bitwise_and(y - bb // NC + NY, NY - 1)
        left = lens[group] - b * PAGE
        cached = ep[i, j, kk, g].astype(F32)
        value = jnp.where(
            lanes < left, cached, jnp.where(lanes < left + SPAN, rolled[i * G_DEV + g], 0.0)
        )
        out_ref[s] = value.astype(BF)
        return carry

    lax.fori_loop(0, pages, page, 0)


def per_device(
    span_q, span_kv, kv_cache, resid, o_weight, norm_gain, w_gate, w_up, w_down, cached_len, page_table
):
    vmem = pl.BlockSpec(memory_space=pltpu.VMEM)
    anywhere = pl.BlockSpec(memory_space=pl.ANY)
    smem = pl.BlockSpec(memory_space=pltpu.SMEM)
    dma = pltpu.SemaphoreType.DMA
    scatter_bufs = [
        pltpu.VMEM((NY, HALF, 1024), BF), pltpu.VMEM((NY, HALF, 1024), BF),
        pltpu.VMEM((NC, HALF, 512), BF), pltpu.VMEM((NC, HALF, 512), BF),
        pltpu.VMEM((NC, HALF, HD), BF), pltpu.VMEM((NC, HALF, HD), BF),
        pltpu.VMEM((NY, HALF, HD), BF), pltpu.VMEM((NY, HALF, HD), BF),
    ]
    every_slot = lax.all_gather(page_table, "grp", axis=0, tiled=True)
    every_len = lax.all_gather(cached_len, "grp", axis=0, tiled=True)
    layer_out, ep, fs = pl.pallas_call(
        layer_kernel,
        out_shape=(
            jax.ShapeDtypeStruct((TOK, HD), BF),
            jax.ShapeDtypeStruct((4, NC, NY, G_DEV, 32, PAGE), BF),
            jax.ShapeDtypeStruct((4, NC, 32, HD), BF),
        ),
        in_specs=[
            vmem, vmem, anywhere, vmem, anywhere, vmem, anywhere, anywhere, anywhere, smem
        ],
        out_specs=(vmem, anywhere, anywhere),
        scratch_shapes=[
            pltpu.VMEM((HD, D), BF),
            pltpu.VMEM((D, FF_DEV), BF),
            pltpu.VMEM((D, FF_DEV), BF),
            pltpu.VMEM((FF_DEV, D), BF),
            pltpu.VMEM((NY, G_DEV, 256, PAGE), BF),
            pltpu.VMEM((G_DEV, HD, SPAN), BF),
            pltpu.VMEM((G_DEV, HD, NC * SPAN), BF),
            pltpu.VMEM((16, 1024), BF),
            pltpu.VMEM((NY, 16, 256), BF),
            pltpu.VMEM((256, HD), BF),
            pltpu.VMEM((G_DEV, NC, HD + 16, SPAN), BF),
            pltpu.VMEM((G_DEV, NC, HD + 16, SPAN), BF),
            pltpu.VMEM((TOK, HD), BF),
            *scatter_bufs,
            *scatter_bufs,
            pltpu.VMEM((NY, HALF, 1024), BF),
            pltpu.VMEM((NY, HALF, 1024), BF),
            pltpu.VMEM((TOK, HD), BF),
            pltpu.VMEM((NC, 8, TOK), F32),
            pltpu.VMEM((NY, 8, TOK), F32),
            pltpu.VMEM((TOK, FF_DEV), BF),
            pltpu.VMEM((8, 128), F32),
            pltpu.VMEM((HALF, HD), F32),
            pltpu.VMEM((HALF, HD), F32),
            dma((4,)), dma((G_DEV,)), dma((2,)),
            dma((NY, G_DEV)), dma((NY, G_DEV)),
            dma((NC,)), dma((NC,)),
            dma((NY,)), dma((NY,)),
            dma((G_DEV, NC)), dma((G_DEV, NC)),
            dma((7, NY)), dma((7, NY)),
            dma((7, NC)), dma((7, NC)),
            dma((NC,)), dma((NC,)),
            dma((NC,)), dma((NC,)),
            dma((4,)), dma((4,)),
            dma((4,)), dma((4,)),
        ],
        compiler_params=pltpu.CompilerParams(
            collective_id=0, has_side_effects=True, vmem_limit_bytes=60 * 1024 * 1024
        ),
        name="layer",
    )(
        span_q, span_kv, kv_cache, resid, o_weight, norm_gain.reshape(1, HD),
        w_gate, w_up, w_down, cached_len,
    )
    pages = page_table.shape[0]
    decode_pool = pl.pallas_call(
        page_kernel,
        out_shape=jax.ShapeDtypeStruct((pages, 32, PAGE), BF),
        in_specs=[vmem, vmem, smem, smem],
        out_specs=vmem,
        scratch_shapes=[
            pltpu.VMEM((12, 32, PAGE), F32),
            pltpu.SMEM((4 * pages,), jnp.int32),
        ],
        compiler_params=pltpu.CompilerParams(vmem_limit_bytes=32 * 1024 * 1024),
        name="pages",
    )(ep, fs, every_slot, every_len)
    return (layer_out, decode_pool)


def solution(mesh):
    in_specs = (
        P("grp", "dev"),
        P("grp", None, "dev"),
        P("grp", None, "dev"),
        P("grp", "dev"),
        P("dev", None),
        P("dev"),
        P(None, "dev"),
        P(None, "dev"),
        P("dev", None),
        P("grp"),
        P("grp"),
    )
    out_specs = (P("grp", "dev"), P("grp", "dev", None))
    return jax.shard_map(
        per_device, mesh=mesh, in_specs=in_specs, out_specs=out_specs, check_vma=False
    )
```

```python
import functools

import jax
import jax.numpy as jnp
from jax import lax
from jax.experimental import pallas as pl
from jax.experimental.pallas import tpu as pltpu
from jax.sharding import PartitionSpec as P

D = 4096
HD = 128
KVH = 4
PAGE = 256
G_DEV = 3
NB = 33
SPAN = 128
NY = 4
NC = 8
TOK = 384
HALF = 192
FF_DEV = 512
PAGES = 99
S_MAX = 8192
NEG = -1e30
SCALE = 1.4426950408889634 / HD**0.5
BF = jnp.bfloat16
F32 = jnp.float32
MESH = pl.DeviceIdType.MESH


def mult(value, by):
    return pl.multiple_of(value, by)


def dot(a, b, dims=(((1,), (0,)), ((), ()))):
    return lax.dot_general(a, b, dims, preferred_element_type=F32)


def layer_kernel(
    q_ref, skv_ref, kv_hbm, resid_ref, ow_hbm, gain_ref, wg_hbm, wu_hbm, wd_hbm, len_ref, table_ref,
    out_ref, pool_ref,
    ow, wg, wu, wd, kv, qt, qg, fr_src, fr, tr, ns, nr, att,
    s1, q1, r1, t1, tr1, z1, zr1, s2, q2, r2, t2, tr2, z2, zr2,
    xs, hm, ss, st, acc_ref, hidden, pair, fin, ep, fs, tb, rolled, plan, plan_smem,
    w_sem, kv_loc, ep_loc,
    kv_s, kv_r, q_s, q_r, f_s, f_r, n_s, n_r, e_s, e_r, t_s, t_r,
    p_s, p_r, l_s, l_r, c_s, c_r, z_s, z_r, ss_s, ss_r, st_s, st_r, g_s, g_r, gt_s, gt_r,
):
    grp = lax.axis_index("grp")
    me = lax.axis_index("dev")
    y = me // NC
    c = lax.rem(me, NC)
    x = lax.rem(me, 4)
    z = lax.rem(me // 4, 2)
    e = me // 4
    core = lax.rem(grp, 2)
    sibling = grp + 1 - 2 * core
    across = lax.rem(grp + 2, 4)

    def y_peer(k):
        return lax.rem(y + k, 4)

    def x_peer(k):
        return lax.rem(x + k, 4)

    def c_peer(j):
        return lax.rem(c + j, NC)

    def e_peer(j):
        return lax.rem(e + j, NC)

    def at_y(k):
        return y_peer(k) * NC + c

    def at_x(k):
        return e * 4 + x_peer(k)

    def at_c(j):
        return y * NC + c_peer(j)

    def at_e(j):
        return e_peer(j) * 4 + x

    def remote(src, dst, send, recv, dev, group=None):
        return pltpu.make_async_remote_copy(
            src_ref=src, dst_ref=dst, send_sem=send, recv_sem=recv,
            device_id=(grp if group is None else group, dev), device_id_type=MESH)

    def loop_c(body):
        def step(j, carry):
            body(j)
            return carry

        lax.fori_loop(1, NC, step, 0)

    barrier = pltpu.get_barrier_semaphore()

    def greet(j):
        pl.semaphore_signal(barrier, inc=1, device_id=(grp, at_c(j)), device_id_type=MESH)
        pl.semaphore_signal(barrier, inc=1, device_id=(grp, at_e(j)), device_id_type=MESH)

    loop_c(greet)
    for other in (sibling, across):
        pl.semaphore_signal(barrier, inc=1, device_id=(other, me), device_id_type=MESH)

    own_kv = [
        pltpu.make_async_copy(
            kv_hbm.at[g, pl.ds(mult(y * 256, 256), 256)], kv.at[0, g], kv_loc.at[g]
        )
        for g in range(G_DEV)
    ]
    for copy in own_kv:
        copy.start()
    for g in range(G_DEV):
        qt[g] = q_ref[g * SPAN : (g + 1) * SPAN, :].astype(F32).T.astype(BF)
    fresh = jnp.zeros((16, 1024), F32)
    for g in range(G_DEV):
        row = lax.broadcasted_iota(jnp.int32, (16, 4), 0)
        col = lax.broadcasted_iota(jnp.int32, (16, 4), 1)
        pick = jnp.where(row == col + 4 * g, 1.0, 0.0).astype(BF)
        fresh = fresh + dot(pick, skv_ref[g])
    fr_src[...] = fresh.astype(BF)
    pl.semaphore_wait(barrier, 2 * (NC - 1) + 2)

    def q_copy(j):
        return remote(
            qt, qg.at[:, :, pl.ds(mult(j * HD, HD), HD)], q_s.at[j], q_r.at[j], at_c(j))

    def f_copy(k):
        return remote(
            fr_src.at[:, pl.ds(mult(y_peer(k) * 256, 256), 256)],
            fr.at[k], f_s.at[k], f_r.at[k], at_y(k))

    def kv_copy(k, g):
        return remote(
            kv_hbm.at[g, pl.ds(mult(y_peer(k) * 256, 256), 256)],
            kv.at[k, g], kv_s.at[k, g], kv_r.at[k, g], at_y(k))

    loop_c(lambda j: q_copy(j).start())
    for k in range(1, 4):
        f_copy(k).start()
    for g in range(G_DEV):
        for k in (1, 3, 2):
            kv_copy(k, g).start()
    weights = [
        pltpu.make_async_copy(src, dst, w_sem.at[i])
        for i, (src, dst) in enumerate(((ow_hbm, ow), (wg_hbm, wg), (wu_hbm, wu), (wd_hbm, wd)))
    ]
    for copy in weights:
        copy.start()
    tb[0] = table_ref[...]
    for g in range(G_DEV):
        qg[g, :, 0:HD] = qt[g]
    fr[0] = fr_src[:, pl.ds(mult(y * 256, 256), 256)]
    for k in range(1, 4):
        f_copy(k).wait_recv()
    fresh_rows = fr[...].reshape(64, 256)
    tr[...] = jnp.concatenate(
        [fresh_rows.astype(F32).T, jnp.zeros((256, 64), F32)], axis=1
    ).astype(BF)

    def t_copy(j):
        return remote(
            tr.at[pl.ds(mult(c_peer(j) * 32, 32), 32), :], fs.at[0, j], t_s.at[j], t_r.at[j], at_c(j))

    loop_c(lambda j: t_copy(j).start())
    fs[0, 0] = tr[pl.ds(mult(c * 32, 32), 32), :]
    loop_c(lambda j: q_copy(j).wait_recv())

    rows = NC * SPAN
    top_dims = (((0,), (0,)), ((), ()))

    def n_copy(g, j):
        return remote(ns.at[g, j], nr.at[g, j], n_s.at[g, j], n_r.at[g, j], at_c(j))

    def e_copy(g, j):
        return remote(
            kv.at[:, g, pl.ds(mult(c_peer(j) * 32, 32), 32), :],
            ep.at[0, g, j], e_s.at[g, j], e_r.at[g, j], at_c(j))

    own_pages = [
        pltpu.make_async_copy(
            kv.at[:, g, pl.ds(mult(c * 32, 32), 32), :], ep.at[0, g, 0], ep_loc.at[g]
        )
        for g in range(G_DEV)
    ]

    for g in range(G_DEV):
        length = len_ref[g]
        high = jnp.full((1, rows), -1e20, F32)
        total = jnp.zeros((1, rows), F32)
        acc = jnp.zeros((HD, rows), F32)

        def block(score, value, high, total, acc):
            new = jnp.maximum(high, jnp.max(score, axis=0, keepdims=True))
            keep = jnp.exp2((high - new) * SCALE)
            weight = jnp.exp2((score - new) * SCALE)
            total = total * keep + jnp.sum(weight, axis=0, keepdims=True)
            acc = acc * keep + dot(value, weight.astype(BF))
            return new, total, acc

        r = lax.broadcasted_iota(jnp.int32, (64, rows), 0)
        token = lax.rem(lax.broadcasted_iota(jnp.int32, (64, rows), 1), SPAN)
        src_y = lax.rem(y - r // 16 + 4, 4)
        r16 = lax.rem(r, 16)
        fresh_at = (src_y * NC + c) * 4 + lax.rem(r16, 4)
        ok = (r16 // 4 == g) & (fresh_at <= token)
        score = dot(fresh_rows[:, 0:HD], qg[g])
        score = jnp.where(ok, score, NEG)
        high, total, acc = block(score, tr[HD : 2 * HD, 0:64], high, total, acc)
        own_kv[g].wait()
        for k in range(1, 4):
            kv_copy(k, g).wait_recv()
        if g < G_DEV - 1:
            loop_c(lambda j, g=g: e_copy(g, j).start())
        for k in range(4):
            first = (lax.rem(y - k + 4, 4) * NC + c) * PAGE
            at = first + lax.broadcasted_iota(jnp.int32, (PAGE, 1), 0)
            score = dot(kv[k, g, 0:HD, :], qg[g], top_dims)
            score = jnp.where(at < length, score, NEG)
            high, total, acc = block(score, kv[k, g, HD : 2 * HD, :], high, total, acc)
        some = total > 0.0
        scaled = acc * jnp.where(some, 1.0 / jnp.where(some, total, 1.0), 0.0)
        level = jnp.where(some, high * SCALE + jnp.log2(jnp.where(some, total, 1.0)), NEG)
        hi = level.astype(BF).astype(F32)
        mid = (level - hi).astype(BF).astype(F32)
        low = level - hi - mid
        which = lax.broadcasted_iota(jnp.int32, (16, rows), 0)
        rest = jnp.where(
            which == 0, hi, jnp.where(which == 1, mid, jnp.where(which == 2, low, 0.0))
        )
        for j in range(NC):
            lanes = slice(j * HD, (j + 1) * HD)
            dest = (NC - j) % NC
            buf = nr if dest == 0 else ns
            buf[g, dest, 0:HD, :] = scaled[:, lanes].astype(BF)
            buf[g, dest, HD : HD + 16, :] = rest[:, lanes].astype(BF)
        loop_c(lambda j, g=g: n_copy(g, j).start())
        if g == G_DEV - 1:
            loop_c(lambda j, g=g: e_copy(g, j).start())
        own_pages[g].start()

    for g in range(G_DEV):
        loop_c(lambda j, g=g: n_copy(g, j).wait_recv())
        levels = [
            jnp.sum(nr[g, j, HD : HD + 16, :].astype(F32), axis=0, keepdims=True) for j in range(NC)
        ]
        top = functools.reduce(jnp.maximum, levels)
        scales = [jnp.exp2(level - top) for level in levels]
        summed = sum(nr[g, j, 0:HD, :].astype(F32) * scales[j] for j in range(NC))
        att[g * SPAN : (g + 1) * SPAN, :] = (summed / sum(scales)).T.astype(BF)

    def g_copy(i, g):
        target = across if i == 2 else sibling
        from_slot = 2 if i == 3 else 0
        return remote(ep.at[from_slot, g], ep.at[i, g], g_s.at[i, g], g_r.at[i, g], me, target)

    def gt_copies(i):
        target = across if i == 2 else sibling
        from_slot = 2 if i == 3 else 0
        return (
            remote(fs.at[from_slot], fs.at[i], gt_s.at[0, i], gt_r.at[0, i], me, target),
            remote(tb.at[from_slot], tb.at[i], gt_s.at[1, i], gt_r.at[1, i], me, target),
        )

    def pages_out(g):
        loop_c(lambda j: e_copy(g, j).wait_recv())
        own_pages[g].wait()
        g_copy(2, g).start()
        g_copy(1, g).start()

    def pages_on(g):
        g_copy(2, g).wait_recv()
        g_copy(3, g).start()

    quarter = HALF // 2
    second_at = (c, e)
    flip_at = (lax.rem(c + 4, NC), e + 1 - 2 * z)
    at_flip = y * NC + lax.rem(c + 4, NC)

    def line(h, k):
        return at_x(k) if h else at_y(k)

    def cross(h, k):
        return at_y(k) if h else at_x(k)

    def strip(part):
        return pl.ds(part * quarter, quarter)

    def scatter(turn, lhs, w, s, q, r, t, tr_, zt, zr, middle):
        def relay(h, side):
            return remote(
                s.at[h, 2, strip(side)], q.at[h, side],
                l_s.at[turn, h, side], l_r.at[turn, h, side], line(h, 1 + 2 * side))

        def first(h, side, part):
            return remote(
                s.at[h, 1 + 2 * side, strip(part)], r.at[h, side, strip(part)],
                p_s.at[turn, h, side, part], p_r.at[turn, h, side, part], line(h, 1 + 2 * side))

        def second(h, k):
            return remote(
                t.at[h, k], tr_.at[h, k], c_s.at[turn, h, k, 0], c_r.at[turn, h, k, 0], cross(h, k))

        def third(h):
            return remote(zt.at[h], zr.at[h], z_s.at[turn, h], z_r.at[turn, h], at_flip)

        def part(h, k):
            left = lhs[h * HALF : (h + 1) * HALF, :]
            if h == 0:
                cols = w[:, pl.ds(mult(y_peer(k) * 1024, 1024), 1024)]
            else:
                cols = jnp.concatenate(
                    [w[:, pl.ds(mult(i * 512 + x_peer(k) * HD, HD), HD)] for i in range(NC)], axis=1
                )
            s[h, k] = dot(left, cols).astype(BF)

        for h in range(2):
            part(h, 2)
            for side in range(2):
                relay(h, side).start()
        for side in range(2):
            for h in range(2):
                part(h, 1 + 2 * side)
                first(h, side, 1 - side).start()
        for side in range(2):
            for h in range(2):
                relay(h, side).wait_recv()
                rows_ = strip(side)
                both = s[h, 1 + 2 * side, rows_].astype(F32) + q[h, side].astype(F32)
                s[h, 1 + 2 * side, rows_] = both.astype(BF)
                first(h, side, side).start()
        for h in range(2):
            part(h, 0)
        middle()

        def summed(h, k):
            if h == 0:
                at = x_peer(k) * HD
                views = [pl.ds(mult(at, HD), HD), pl.ds(mult(at + 512, HD), HD)]
            else:
                views = [pl.ds(mult(y_peer(k) * 256, 256), 256)]
            blocks = [
                s[h, 0, :, v].astype(F32) + r[h, 0, :, v].astype(F32) + r[h, 1, :, v].astype(F32)
                for v in views
            ]
            return blocks[0] if h else jnp.concatenate(blocks, axis=1)

        for h in range(2):
            for side in range(2):
                for part_ in range(2):
                    first(h, side, part_).wait_recv()
            for k in (1, 3, 2):
                t[h, k] = summed(h, k).astype(BF)
                second(h, k).start()
        mine, other = pl.ds(mult(z * HD, HD), HD), pl.ds(mult((1 - z) * HD, HD), HD)
        for h in range(2):
            pair[h] = summed(h, 0)
        for h in range(2):
            for k in (1, 3, 2):
                second(h, k).wait_recv()
            total = pair[h]
            for k in range(1, 4):
                total = total + tr_[h, k].astype(F32)
            pair[h] = total
            zt[h] = pair[h, :, other].astype(BF)
            third(h).start()
        for h in range(2):
            third(h).wait_recv()
            fin[h] = pair[h, :, mine] + zr[h].astype(F32)

        def finish():
            for h in range(2):
                third(h).wait_send()
                for side in range(2):
                    relay(h, side).wait_send()
                    for part_ in range(2):
                        first(h, side, part_).wait_send()
                for k in range(1, 4):
                    second(h, k).wait_send()

        return finish

    weights[0].wait()

    def middle_1():
        loop_c(lambda j: t_copy(j).wait_recv())
        for copy in gt_copies(2) + gt_copies(1):
            copy.start()
        for g in range(G_DEV):
            pages_out(g)

    finish_1 = scatter(0, att, ow, s1, q1, r1, t1, tr1, z1, zr1, middle_1)

    ones = jnp.ones((8, HD), F32)
    for h in range(2):
        span = slice(h * HALF, (h + 1) * HALF)
        mid_bf = (resid_ref[span, :].astype(F32) + fin[h]).astype(BF)
        hm[span, :] = mid_bf
        wide = mid_bf.astype(F32)
        xs[h, x if h else y, :, pl.ds(mult(second_at[h] * HD, HD), HD)] = (
            wide * gain_ref[...]
        ).astype(BF)

    prime = (y, x)

    def x_flip(h):
        view = xs.at[h, prime[h], :, pl.ds(mult(second_at[h] * HD, HD), HD)]
        return remote(view, view, z_s.at[2, h], z_r.at[2, h], at_flip)

    def x_cross(h, k, n):
        at = flip_at[h] if n else second_at[h]
        view = xs.at[h, prime[h], :, pl.ds(mult(at * HD, HD), HD)]
        return remote(view, view, c_s.at[2, h, k, n], c_r.at[2, h, k, n], cross(h, k))

    def x_line(h, side, part):
        view = xs.at[h, prime[h], strip(part)]
        return remote(
            view, view, p_s.at[2, h, side, part], p_r.at[2, h, side, part], line(h, 1 + 2 * side))

    def x_relay(h, side):
        view = xs.at[h, lax.rem(prime[h] + 3 - 2 * side, 4), strip(side)]
        return remote(
            view, view, l_s.at[2, h, side], l_r.at[2, h, side], line(h, 1 + 2 * side))

    def ss1(j):
        return remote(ss.at[0], ss.at[j], ss_s.at[j], ss_r.at[j], at_c(j))

    def st1(k):
        return remote(st.at[0], st.at[k], st_s.at[k], st_r.at[k], at_y(k))

    for h in range(2):
        x_flip(h).start()
        for k in (1, 3, 2):
            x_cross(h, k, 0).start()
    wide = hm[...].astype(F32)
    ss[0] = lax.dot_general(
        ones, wide * wide, (((1,), (1,)), ((), ())),
        precision=lax.Precision.HIGHEST, preferred_element_type=F32)
    loop_c(lambda j: ss1(j).start())
    for h in range(2):
        x_flip(h).wait_recv()
        for k in (1, 3, 2):
            x_cross(h, k, 1).start()
    for h in range(2):
        for n in range(2):
            for k in range(1, 4):
                x_cross(h, k, n).wait_recv()
        for n in range(2):
            for side in range(2):
                x_line(h, side, (side + n) % 2).start()
    loop_c(lambda j: ss1(j).wait_recv())
    st[0] = jnp.sum(ss[...], axis=0)
    for k in range(1, 4):
        st1(k).start()

    weights[1].wait()
    weights[2].wait()
    for k in (0, 1, 3, 2):
        for h in range(2):
            if k == 2:
                x_relay(h, 0).wait_recv()
                x_relay(h, 1).wait_recv()
            elif k:
                x_line(h, k // 2, 1 - k // 2).wait_recv()
            if h == 0:
                at = lax.rem(y - k + 4, 4)
                deep = pl.ds(mult(at * 1024, 1024), 1024)
                gates, ups = wg[deep, :], wu[deep, :]
            else:
                at = lax.rem(x - k + 4, 4)
                deep = [pl.ds(mult(i * 512 + at * HD, HD), HD) for i in range(NC)]
                gates = jnp.concatenate([wg[d, :] for d in deep], axis=0)
                ups = jnp.concatenate([wu[d, :] for d in deep], axis=0)
            if k:
                acc_ref[h, 0] += dot(xs[h, at], gates)
                acc_ref[h, 1] += dot(xs[h, at], ups)
            else:
                acc_ref[h, 0] = dot(xs[h, at], gates)
                acc_ref[h, 1] = dot(xs[h, at], ups)
        if k == 0:
            for side in range(2):
                for h in range(2):
                    x_line(h, side, side).wait_recv()
                    x_relay(h, side).start()
        if k == 1:
            for g in range(2):
                pages_on(g)
            for copy in gt_copies(2):
                copy.wait_recv()
            for copy in gt_copies(3):
                copy.start()
            for kk in range(1, 4):
                st1(kk).wait_recv()
    squares = jnp.sum(st[...], axis=0)
    factor = lax.rsqrt(squares * (1.0 / D) + 1e-5)
    factor = jnp.broadcast_to(factor[0:1, :], (HD, TOK)).T
    for h in range(2):
        span = slice(h * HALF, (h + 1) * HALF)
        scale = factor[span, 0:1]
        gate = acc_ref[h, 0] * scale
        upward = acc_ref[h, 1] * scale
        hidden[span, :] = (gate / (1.0 + jnp.exp(-gate)) * upward).astype(BF)

    lane = lax.broadcasted_iota(jnp.int32, (HD, 1), 0)

    def roll_group(i, carry):
        fk = lane // 16
        r16 = lax.rem(lane, 16)
        column = lax.broadcasted_iota(jnp.int32, (HD, G_DEV * SPAN), 1)
        spans = jnp.zeros((32, G_DEV * SPAN), F32)
        for j in range(NC):
            from_c = lax.rem(c - j + NC, NC)
            token = (lax.rem(y - fk + 8, 4) * NC + from_c) * 4 + lax.rem(r16, 4)
            target = jnp.where((lane < 64) & (r16 < 12), (r16 // 4) * SPAN + token, -1)
            pick = jnp.where(column == target, 1.0, 0.0).astype(BF)
            spans = spans + dot(fs[i, j], pick)
        spans = spans.astype(BF)
        wide_column = lax.broadcasted_iota(jnp.int32, (SPAN, PAGE), 1)
        for g in range(G_DEV):
            at = lane + tb[i, PAGES + g : PAGES + g + 1, 0:1]
            spin = jnp.where(wide_column == lax.rem(at, PAGE), 1.0, 0.0).astype(BF)
            rolled[i * G_DEV + g] = dot(spans[:, g * SPAN : (g + 1) * SPAN], spin)
        return carry

    def pages_in():
        pages_on(2)
        for i in (1, 3):
            for copy in gt_copies(i):
                copy.wait_recv()
        lax.fori_loop(0, 4, roll_group, 0)
        page = lax.broadcasted_iota(jnp.int32, (HD, 1), 0)
        gl = jnp.where(page >= NB, 1, 0) + jnp.where(page >= 2 * NB, 1, 0)
        b = page - gl * NB
        bb = jnp.minimum(b, 31)
        jj = lax.rem(c - bb + 32, NC)
        kk = lax.rem(y - bb // NC + 4, 4)
        slot = grp * PAGES + lax.broadcasted_iota(jnp.int32, (HD, HD), 1)
        where_ep = jnp.zeros((HD, HD), jnp.int32)
        where_left = jnp.full((HD, HD), -S_MAX, jnp.int32)
        where_roll = jnp.zeros((HD, HD), jnp.int32)
        for i in range(4):
            length = jnp.where(
                gl == 0,
                tb[i, PAGES : PAGES + 1, 0:1],
                jnp.where(gl == 1, tb[i, PAGES + 1 : PAGES + 2, 0:1], tb[i, PAGES + 2 : PAGES + 3, 0:1]),
            )
            match = (tb[i] == slot) & (page < PAGES)
            where_ep = jnp.where(match, ((i * G_DEV + gl) * NC + jj) * 4 + kk, where_ep)
            where_left = jnp.where(match, length - b * PAGE, where_left)
            where_roll = jnp.where(match, i * G_DEV + gl, where_roll)
        for n, table in enumerate((where_ep, where_left, where_roll)):
            plan[n] = jnp.broadcast_to(jnp.max(table, axis=0, keepdims=True), (8, HD))
        to_smem = pltpu.make_async_copy(plan, plan_smem, ep_loc.at[G_DEV])
        to_smem.start()
        for i in (1, 3):
            for g in range(G_DEV):
                g_copy(i, g).wait_recv()
        to_smem.wait()
        lanes = lax.broadcasted_iota(jnp.int32, (1, PAGE), 1)
        flat = ep.reshape(4 * G_DEV * NC * 4, 32, PAGE)

        def one_page(s, carry):
            left = plan_smem[1, 0, s]
            cached = flat[plan_smem[0, 0, s]].astype(F32)
            value = jnp.where(
                lanes < left,
                cached,
                jnp.where(lanes < left + SPAN, rolled[plan_smem[2, 0, s]], 0.0),
            )
            pool_ref[s] = value.astype(BF)
            return carry

        lax.fori_loop(0, PAGES, one_page, 0)

    weights[3].wait()
    finish_2 = scatter(1, hidden, wd, s2, q2, r2, t2, tr2, z2, zr2, pages_in)
    for h in range(2):
        span = slice(h * HALF, (h + 1) * HALF)
        out_ref[span, :] = (hm[span, :].astype(F32) + fin[h]).astype(BF)

    for i in (1, 2, 3):
        for g in range(G_DEV):
            g_copy(i, g).wait_send()
        for copy in gt_copies(i):
            copy.wait_send()
    finish_1()
    finish_2()
    for h in range(2):
        x_flip(h).wait_send()
        for side in range(2):
            x_relay(h, side).wait_send()
            for part_ in range(2):
                x_line(h, side, part_).wait_send()
        for k in range(1, 4):
            for n in range(2):
                x_cross(h, k, n).wait_send()
    for k in range(1, 4):
        f_copy(k).wait_send()
        st1(k).wait_send()
        for g in range(G_DEV):
            kv_copy(k, g).wait_send()

    def sent(j):
        q_copy(j).wait_send()
        t_copy(j).wait_send()
        ss1(j).wait_send()
        for g in range(G_DEV):
            n_copy(g, j).wait_send()
            e_copy(g, j).wait_send()

    loop_c(sent)


def per_device(
    span_q, span_kv, kv_cache, resid, o_weight, norm_gain, w_gate, w_up, w_down, cached_len, page_table
):
    vmem = pl.BlockSpec(memory_space=pltpu.VMEM)
    anywhere = pl.BlockSpec(memory_space=pl.ANY)
    smem = pl.BlockSpec(memory_space=pltpu.SMEM)
    dma = pltpu.SemaphoreType.DMA
    scatter_bufs = [
        pltpu.VMEM((2, 4, HALF, 1024), BF), pltpu.VMEM((2, 2, HALF // 2, 1024), BF),
        pltpu.VMEM((2, 2, HALF, 1024), BF),
        pltpu.VMEM((2, 4, HALF, 2 * HD), BF), pltpu.VMEM((2, 4, HALF, 2 * HD), BF),
        pltpu.VMEM((2, HALF, HD), BF), pltpu.VMEM((2, HALF, HD), BF),
    ]
    table = jnp.concatenate([page_table, cached_len, jnp.zeros((HD - PAGES - G_DEV,), jnp.int32)])
    table = jnp.broadcast_to(table[:, None], (HD, HD))
    layer_out, decode_pool = pl.pallas_call(
        layer_kernel,
        out_shape=(
            jax.ShapeDtypeStruct((TOK, HD), BF),
            jax.ShapeDtypeStruct((PAGES, 32, PAGE), BF),
        ),
        in_specs=[
            vmem, vmem, anywhere, vmem, anywhere, vmem, anywhere, anywhere, anywhere, smem, vmem
        ],
        out_specs=(vmem, vmem),
        scratch_shapes=[
            pltpu.VMEM((HD, D), BF),
            pltpu.VMEM((D, FF_DEV), BF),
            pltpu.VMEM((D, FF_DEV), BF),
            pltpu.VMEM((FF_DEV, D), BF),
            pltpu.VMEM((4, G_DEV, 256, PAGE), BF),
            pltpu.VMEM((G_DEV, HD, SPAN), BF),
            pltpu.VMEM((G_DEV, HD, NC * SPAN), BF),
            pltpu.VMEM((16, 1024), BF),
            pltpu.VMEM((4, 16, 256), BF),
            pltpu.VMEM((256, HD), BF),
            pltpu.VMEM((G_DEV, NC, HD + 16, SPAN), BF),
            pltpu.VMEM((G_DEV, NC, HD + 16, SPAN), BF),
            pltpu.VMEM((TOK, HD), BF),
            *scatter_bufs,
            *scatter_bufs,
            pltpu.VMEM((2, 4, HALF, 1024), BF),
            pltpu.VMEM((TOK, HD), BF),
            pltpu.VMEM((NC, 8, TOK), F32),
            pltpu.VMEM((4, 8, TOK), F32),
            pltpu.VMEM((2, 2, HALF, FF_DEV), F32),
            pltpu.VMEM((TOK, FF_DEV), BF),
            pltpu.VMEM((2, HALF, 2 * HD), F32),
            pltpu.VMEM((2, HALF, HD), F32),
            pltpu.VMEM((4, G_DEV, NC, 4, 32, PAGE), BF),
            pltpu.VMEM((4, NC, 32, HD), BF),
            pltpu.VMEM((4, HD, HD), jnp.int32),
            pltpu.VMEM((4 * G_DEV, 32, PAGE), F32),
            pltpu.VMEM((3, 8, HD), jnp.int32),
            pltpu.SMEM((3, 8, HD), jnp.int32),
            dma((4,)), dma((G_DEV,)), dma((G_DEV + 1,)),
            dma((4, G_DEV)), dma((4, G_DEV)),
            dma((NC,)), dma((NC,)),
            dma((4,)), dma((4,)),
            dma((G_DEV, NC)), dma((G_DEV, NC)),
            dma((G_DEV, NC)), dma((G_DEV, NC)),
            dma((NC,)), dma((NC,)),
            dma((3, 2, 2, 2)), dma((3, 2, 2, 2)),
            dma((3, 2, 2)), dma((3, 2, 2)),
            dma((3, 2, 4, 2)), dma((3, 2, 4, 2)),
            dma((3, 2)), dma((3, 2)),
            dma((NC,)), dma((NC,)),
            dma((4,)), dma((4,)),
            dma((4, G_DEV)), dma((4, G_DEV)),
            dma((2, 4)), dma((2, 4)),
        ],
        compiler_params=pltpu.CompilerParams(
            collective_id=0, has_side_effects=True, vmem_limit_bytes=60 * 1024 * 1024
        ),
        name="layer",
    )(
        span_q, span_kv.transpose(0, 2, 1), kv_cache, resid, o_weight, norm_gain.reshape(1, HD),
        w_gate, w_up, w_down, cached_len, table,
    )
    return (layer_out, decode_pool)


def solution(mesh):
    in_specs = (
        P("grp", "dev"),
        P("grp", None, "dev"),
        P("grp", None, "dev"),
        P("grp", "dev"),
        P("dev", None),
        P("dev"),
        P(None, "dev"),
        P(None, "dev"),
        P("dev", None),
        P("grp"),
        P("grp"),
    )
    out_specs = (P("grp", "dev"), P("grp", "dev", None))
    return jax.shard_map(
        per_device, mesh=mesh, in_specs=in_specs, out_specs=out_specs, check_vma=False
    )
```

```python
import functools

import jax
import jax.numpy as jnp
from jax import lax
from jax.experimental import pallas as pl
from jax.experimental.pallas import tpu as pltpu
from jax.sharding import PartitionSpec as P

D = 4096
HD = 128
KVH = 4
PAGE = 256
G_DEV = 3
NB = 33
SPAN = 128
NY = 4
NC = 8
TOK = 384
HALF = 192
FF_DEV = 512
PAGES = 99
S_MAX = 8192
NEG = -1e30
SCALE = 1.4426950408889634 / HD**0.5
BF = jnp.bfloat16
F32 = jnp.float32
MESH = pl.DeviceIdType.MESH


def mult(value, by):
    return pl.multiple_of(value, by)


def dot(a, b, dims=(((1,), (0,)), ((), ()))):
    return lax.dot_general(a, b, dims, preferred_element_type=F32)


def layer_kernel(
    q_ref, skv_ref, kv_hbm, resid_ref, ow_hbm, gain_ref, wg_hbm, wu_hbm, wd_hbm, len_ref, table_ref,
    out_ref, pool_ref,
    ow, wg, wu, wd, kv, qt, qg, fr_src, fr, tr, ns, nr, ms, mr, att,
    s1, q1, r1, t1, tr1, z1, zr1, s2, q2, r2, t2, tr2, z2, zr2,
    xs, hm, ss, st, acc_ref, hidden, pair, fin, ep, fs, tb, rolled, plan, plan_smem,
    w_sem, kv_loc, ep_loc,
    kv_s, kv_r, q_s, q_r, f_s, f_r, n_s, n_r, m_s, m_r, e_s, e_r, t_s, t_r,
    p_s, p_r, l_s, l_r, c_s, c_r, z_s, z_r, ss_s, ss_r, st_s, st_r, g_s, g_r, gt_s, gt_r,
):
    grp = lax.axis_index("grp")
    me = lax.axis_index("dev")
    y = me // NC
    c = lax.rem(me, NC)
    x = lax.rem(me, 4)
    z = lax.rem(me // 4, 2)
    e = me // 4
    core = lax.rem(grp, 2)
    sibling = grp + 1 - 2 * core
    across = lax.rem(grp + 2, 4)

    def y_peer(k):
        return lax.rem(y + k, 4)

    def x_peer(k):
        return lax.rem(x + k, 4)

    def c_peer(j):
        return lax.rem(c + j, NC)

    def at_y(k):
        return y_peer(k) * NC + c

    def at_x(k):
        return e * 4 + x_peer(k)

    def at_c(j):
        return y * NC + c_peer(j)

    def remote(src, dst, send, recv, dev, group=None):
        return pltpu.make_async_remote_copy(
            src_ref=src, dst_ref=dst, send_sem=send, recv_sem=recv,
            device_id=(grp if group is None else group, dev), device_id_type=MESH)

    def loop_c(body):
        def step(j, carry):
            body(j)
            return carry

        lax.fori_loop(1, NC, step, 0)

    barrier = pltpu.get_barrier_semaphore()

    def greet(j):
        pl.semaphore_signal(barrier, inc=1, device_id=(grp, at_c(j)), device_id_type=MESH)

    loop_c(greet)
    for k in range(1, 4):
        pl.semaphore_signal(barrier, inc=1, device_id=(grp, at_y(k)), device_id_type=MESH)
    for other in (sibling, across):
        pl.semaphore_signal(barrier, inc=1, device_id=(other, me), device_id_type=MESH)

    own_kv = [
        pltpu.make_async_copy(
            kv_hbm.at[g, pl.ds(mult(y * 256, 256), 256)], kv.at[0, g], kv_loc.at[g]
        )
        for g in range(G_DEV)
    ]
    for copy in own_kv:
        copy.start()
    for g in range(G_DEV):
        qt[g] = q_ref[g * SPAN : (g + 1) * SPAN, :].astype(F32).T.astype(BF)
    fresh = jnp.zeros((16, 1024), F32)
    for g in range(G_DEV):
        row = lax.broadcasted_iota(jnp.int32, (16, 4), 0)
        col = lax.broadcasted_iota(jnp.int32, (16, 4), 1)
        pick = jnp.where(row == col + 4 * g, 1.0, 0.0).astype(BF)
        fresh = fresh + dot(pick, skv_ref[g])
    fr_src[...] = fresh.astype(BF)
    pl.semaphore_wait(barrier, NC - 1 + 3 + 2)
    at_flip = y * NC + lax.rem(c + 4, NC)

    def q_lanes(slot):
        return qg.at[:, :, pl.ds(slot * HD, HD)]

    def q_copy(n, k):
        src = q_lanes(4) if n and k else qt
        return remote(
            src, q_lanes(n * 4 + k), q_s.at[n * 4 + k], q_r.at[n * 4 + k],
            at_x(k) if k else at_flip)

    def f_copy(k):
        return remote(
            fr_src.at[:, pl.ds(mult(y_peer(k) * 256, 256), 256)],
            fr.at[k], f_s.at[k], f_r.at[k], at_y(k))

    def kv_copy(k, g):
        return remote(
            kv_hbm.at[g, pl.ds(mult(y_peer(k) * 256, 256), 256)],
            kv.at[k, g], kv_s.at[k, g], kv_r.at[k, g], at_y(k))

    q_copy(1, 0).start()
    for k in (1, 3, 2):
        q_copy(0, k).start()
    for k in range(1, 4):
        f_copy(k).start()
    for g in range(G_DEV):
        for k in (1, 3, 2):
            kv_copy(k, g).start()
    weights = [
        pltpu.make_async_copy(src, dst, w_sem.at[i])
        for i, (src, dst) in enumerate(((ow_hbm, ow), (wg_hbm, wg), (wu_hbm, wu), (wd_hbm, wd)))
    ]
    for copy in weights:
        copy.start()
    q_copy(1, 0).wait_recv()
    for k in (1, 3, 2):
        q_copy(1, k).start()
    tb[0] = table_ref[...]
    for g in range(G_DEV):
        qg[g, :, 0:HD] = qt[g]
    fr[0] = fr_src[:, pl.ds(mult(y * 256, 256), 256)]
    for k in range(1, 4):
        f_copy(k).wait_recv()
    fresh_rows = fr[...].reshape(64, 256)
    tr[...] = jnp.concatenate(
        [fresh_rows.astype(F32).T, jnp.zeros((256, 64), F32)], axis=1
    ).astype(BF)

    def t_copy(j):
        return remote(
            tr.at[pl.ds(mult(c_peer(j) * 32, 32), 32), :], fs.at[0, j], t_s.at[j], t_r.at[j], at_c(j))

    loop_c(lambda j: t_copy(j).start())
    fs[0, 0] = tr[pl.ds(mult(c * 32, 32), 32), :]
    for k in range(1, 4):
        for n in range(2):
            q_copy(n, k).wait_recv()

    rows = NC * SPAN
    top_dims = (((0,), (0,)), ((), ()))

    def n_copy(g, k):
        return remote(ns.at[g, k], nr.at[g, k], n_s.at[g, k], n_r.at[g, k], at_x(k))

    def m_copy(g):
        return remote(ms.at[g], mr.at[g], m_s.at[g], m_r.at[g], at_flip)

    def level_rows(level):
        hi = level.astype(BF).astype(F32)
        mid = (level - hi).astype(BF).astype(F32)
        low = level - hi - mid
        which = lax.broadcasted_iota(jnp.int32, (16, level.shape[1]), 0)
        return jnp.where(
            which == 0, hi, jnp.where(which == 1, mid, jnp.where(which == 2, low, 0.0))
        )

    def merge(parts):
        levels = [jnp.sum(p[HD : HD + 16, :].astype(F32), axis=0, keepdims=True) for p in parts]
        top = functools.reduce(jnp.maximum, levels)
        scales = [jnp.exp2(level - top) for level in levels]
        total = sum(scales)
        summed = sum(p[0:HD, :].astype(F32) * scale for p, scale in zip(parts, scales))
        return summed / total, top + jnp.log2(total)

    def merge_other(g):
        for k in range(1, 4):
            n_copy(g, k).wait_recv()
        value, level = merge([nr[g, k, 1] for k in range(4)])
        ms[g, 0:HD, :] = value.astype(BF)
        ms[g, HD : HD + 16, :] = level_rows(level).astype(BF)
        m_copy(g).start()

    def e_copy(g, j):
        return remote(
            kv.at[:, g, pl.ds(mult(c_peer(j) * 32, 32), 32), :],
            ep.at[0, g, j], e_s.at[g, j], e_r.at[g, j], at_c(j))

    own_pages = [
        pltpu.make_async_copy(
            kv.at[:, g, pl.ds(mult(c * 32, 32), 32), :], ep.at[0, g, 0], ep_loc.at[g]
        )
        for g in range(G_DEV)
    ]

    for g in range(G_DEV):
        length = len_ref[g]
        high = jnp.full((1, rows), -1e20, F32)
        total = jnp.zeros((1, rows), F32)
        acc = jnp.zeros((HD, rows), F32)

        def block(score, value, high, total, acc):
            new = jnp.maximum(high, jnp.max(score, axis=0, keepdims=True))
            keep = jnp.exp2((high - new) * SCALE)
            weight = jnp.exp2((score - new) * SCALE)
            total = total * keep + jnp.sum(weight, axis=0, keepdims=True)
            acc = acc * keep + dot(value, weight.astype(BF))
            return new, total, acc

        r = lax.broadcasted_iota(jnp.int32, (64, rows), 0)
        token = lax.rem(lax.broadcasted_iota(jnp.int32, (64, rows), 1), SPAN)
        src_y = lax.rem(y - r // 16 + 4, 4)
        r16 = lax.rem(r, 16)
        fresh_at = (src_y * NC + c) * 4 + lax.rem(r16, 4)
        ok = (r16 // 4 == g) & (fresh_at <= token)
        score = dot(fresh_rows[:, 0:HD], qg[g])
        score = jnp.where(ok, score, NEG)
        high, total, acc = block(score, tr[HD : 2 * HD, 0:64], high, total, acc)
        own_kv[g].wait()
        for k in range(1, 4):
            kv_copy(k, g).wait_recv()
        if g < G_DEV - 1:
            loop_c(lambda j, g=g: e_copy(g, j).start())
        for k in range(4):
            first = (lax.rem(y - k + 4, 4) * NC + c) * PAGE
            at = first + lax.broadcasted_iota(jnp.int32, (PAGE, 1), 0)
            score = dot(kv[k, g, 0:HD, :], qg[g], top_dims)
            score = jnp.where(at < length, score, NEG)
            high, total, acc = block(score, kv[k, g, HD : 2 * HD, :], high, total, acc)
        some = total > 0.0
        scaled = acc * jnp.where(some, 1.0 / jnp.where(some, total, 1.0), 0.0)
        level = jnp.where(some, high * SCALE + jnp.log2(jnp.where(some, total, 1.0)), NEG)
        rest = level_rows(level)
        for n in range(2):
            for k in range(4):
                lanes = slice((n * 4 + k) * HD, (n * 4 + k + 1) * HD)
                buf = ns if k else nr
                buf[g, (4 - k) % 4, n, 0:HD, :] = scaled[:, lanes].astype(BF)
                buf[g, (4 - k) % 4, n, HD : HD + 16, :] = rest[:, lanes].astype(BF)
        for k in (1, 3, 2):
            n_copy(g, k).start()
        if g == G_DEV - 1:
            loop_c(lambda j, g=g: e_copy(g, j).start())
        own_pages[g].start()
        if g:
            merge_other(g - 1)

    merge_other(G_DEV - 1)
    for g in range(G_DEV):
        m_copy(g).wait_recv()
        value, _ = merge([nr[g, k, 0] for k in range(4)] + [mr[g]])
        att[g * SPAN : (g + 1) * SPAN, :] = value.T.astype(BF)

    def g_copy(i, g):
        target = across if i == 2 else sibling
        from_slot = 2 if i == 3 else 0
        return remote(ep.at[from_slot, g], ep.at[i, g], g_s.at[i, g], g_r.at[i, g], me, target)

    def gt_copies(i):
        target = across if i == 2 else sibling
        from_slot = 2 if i == 3 else 0
        return (
            remote(fs.at[from_slot], fs.at[i], gt_s.at[0, i], gt_r.at[0, i], me, target),
            remote(tb.at[from_slot], tb.at[i], gt_s.at[1, i], gt_r.at[1, i], me, target),
        )

    def pages_out(g):
        loop_c(lambda j: e_copy(g, j).wait_recv())
        own_pages[g].wait()
        g_copy(2, g).start()
        g_copy(1, g).start()

    def pages_on(g):
        g_copy(2, g).wait_recv()
        g_copy(3, g).start()

    quarter = HALF // 2
    second_at = (c, e)
    flip_at = (lax.rem(c + 4, NC), e + 1 - 2 * z)

    def line(h, k):
        return at_x(k) if h else at_y(k)

    def cross(h, k):
        return at_y(k) if h else at_x(k)

    def strip(part):
        return pl.ds(part * quarter, quarter)

    def scatter(turn, lhs, w, s, q, r, t, tr_, zt, zr, middle, later):
        def relay(h, side):
            return remote(
                s.at[h, 2, strip(side)], q.at[h, side],
                l_s.at[turn, h, side], l_r.at[turn, h, side], line(h, 1 + 2 * side))

        def first(h, side, part):
            return remote(
                s.at[h, 1 + 2 * side, strip(part)], r.at[h, side, strip(part)],
                p_s.at[turn, h, side, part], p_r.at[turn, h, side, part], line(h, 1 + 2 * side))

        def second(h, k):
            return remote(
                t.at[h, k], tr_.at[h, k], c_s.at[turn, h, k, 0], c_r.at[turn, h, k, 0], cross(h, k))

        def third(h):
            return remote(zt.at[h], zr.at[h], z_s.at[turn, h], z_r.at[turn, h], at_flip)

        def part(h, k):
            left = lhs[h * HALF : (h + 1) * HALF, :]
            if h == 0:
                cols = w[:, pl.ds(mult(y_peer(k) * 1024, 1024), 1024)]
            else:
                cols = jnp.concatenate(
                    [w[:, pl.ds(mult(i * 512 + x_peer(k) * HD, HD), HD)] for i in range(NC)], axis=1
                )
            s[h, k] = dot(left, cols).astype(BF)

        for h in range(2):
            part(h, 2)
            for side in range(2):
                relay(h, side).start()
        for side in range(2):
            for h in range(2):
                part(h, 1 + 2 * side)
                first(h, side, 1 - side).start()
        for side in range(2):
            for h in range(2):
                relay(h, side).wait_recv()
                rows_ = strip(side)
                both = s[h, 1 + 2 * side, rows_].astype(F32) + q[h, side].astype(F32)
                s[h, 1 + 2 * side, rows_] = both.astype(BF)
                first(h, side, side).start()
        for h in range(2):
            part(h, 0)
        middle()

        def summed(h, k):
            if h == 0:
                at = x_peer(k) * HD
                views = [pl.ds(mult(at, HD), HD), pl.ds(mult(at + 512, HD), HD)]
            else:
                views = [pl.ds(mult(y_peer(k) * 256, 256), 256)]
            blocks = [
                s[h, 0, :, v].astype(F32) + r[h, 0, :, v].astype(F32) + r[h, 1, :, v].astype(F32)
                for v in views
            ]
            return blocks[0] if h else jnp.concatenate(blocks, axis=1)

        for h in range(2):
            for side in range(2):
                for part_ in range(2):
                    first(h, side, part_).wait_recv()
            for k in (1, 3, 2):
                t[h, k] = summed(h, k).astype(BF)
                second(h, k).start()
        later()
        mine, other = pl.ds(mult(z * HD, HD), HD), pl.ds(mult((1 - z) * HD, HD), HD)
        for h in range(2):
            pair[h] = summed(h, 0)
        for h in range(2):
            for k in (1, 3, 2):
                second(h, k).wait_recv()
            total = pair[h]
            for k in range(1, 4):
                total = total + tr_[h, k].astype(F32)
            pair[h] = total
            zt[h] = pair[h, :, other].astype(BF)
            third(h).start()
        for h in range(2):
            third(h).wait_recv()
            fin[h] = pair[h, :, mine] + zr[h].astype(F32)

        def finish():
            for h in range(2):
                third(h).wait_send()
                for side in range(2):
                    relay(h, side).wait_send()
                    for part_ in range(2):
                        first(h, side, part_).wait_send()
                for k in range(1, 4):
                    second(h, k).wait_send()

        return finish

    weights[0].wait()

    def middle_1():
        loop_c(lambda j: t_copy(j).wait_recv())
        for copy in gt_copies(2) + gt_copies(1):
            copy.start()
        pages_out(0)

    finish_1 = scatter(0, att, ow, s1, q1, r1, t1, tr1, z1, zr1, middle_1, lambda: None)

    ones = jnp.ones((8, HD), F32)
    for h in range(2):
        span = slice(h * HALF, (h + 1) * HALF)
        mid_bf = (resid_ref[span, :].astype(F32) + fin[h]).astype(BF)
        hm[span, :] = mid_bf
        wide = mid_bf.astype(F32)
        xs[h, x if h else y, :, pl.ds(mult(second_at[h] * HD, HD), HD)] = (
            wide * gain_ref[...]
        ).astype(BF)

    prime = (y, x)

    def x_flip(h):
        view = xs.at[h, prime[h], :, pl.ds(mult(second_at[h] * HD, HD), HD)]
        return remote(view, view, z_s.at[2, h], z_r.at[2, h], at_flip)

    def x_cross(h, k, n):
        at = flip_at[h] if n else second_at[h]
        view = xs.at[h, prime[h], :, pl.ds(mult(at * HD, HD), HD)]
        return remote(view, view, c_s.at[2, h, k, n], c_r.at[2, h, k, n], cross(h, k))

    def x_line(h, side, part):
        view = xs.at[h, prime[h], strip(part)]
        return remote(
            view, view, p_s.at[2, h, side, part], p_r.at[2, h, side, part], line(h, 1 + 2 * side))

    def x_relay(h, side):
        view = xs.at[h, lax.rem(prime[h] + 3 - 2 * side, 4), strip(side)]
        return remote(
            view, view, l_s.at[2, h, side], l_r.at[2, h, side], line(h, 1 + 2 * side))

    def ss1(j):
        return remote(ss.at[0], ss.at[j], ss_s.at[j], ss_r.at[j], at_c(j))

    def st1(k):
        return remote(st.at[0], st.at[k], st_s.at[k], st_r.at[k], at_y(k))

    for h in range(2):
        x_flip(h).start()
        for k in (1, 3, 2):
            x_cross(h, k, 0).start()
    wide = hm[...].astype(F32)
    ss[0] = lax.dot_general(
        ones, wide * wide, (((1,), (1,)), ((), ())),
        precision=lax.Precision.HIGHEST, preferred_element_type=F32)
    loop_c(lambda j: ss1(j).start())
    for h in range(2):
        x_flip(h).wait_recv()
        for k in (1, 3, 2):
            x_cross(h, k, 1).start()
    pages_out(1)
    for h in range(2):
        for n in range(2):
            for k in range(1, 4):
                x_cross(h, k, n).wait_recv()
        for n in range(2):
            for side in range(2):
                x_line(h, side, (side + n) % 2).start()
    pages_out(2)
    loop_c(lambda j: ss1(j).wait_recv())
    st[0] = jnp.sum(ss[...], axis=0)
    for k in range(1, 4):
        st1(k).start()

    weights[1].wait()
    weights[2].wait()
    for k in (0, 1, 3, 2):
        for h in range(2):
            if k == 2:
                x_relay(h, 0).wait_recv()
                x_relay(h, 1).wait_recv()
            elif k:
                x_line(h, k // 2, 1 - k // 2).wait_recv()
            if h == 0:
                at = lax.rem(y - k + 4, 4)
                deep = pl.ds(mult(at * 1024, 1024), 1024)
                gates, ups = wg[deep, :], wu[deep, :]
            else:
                at = lax.rem(x - k + 4, 4)
                deep = [pl.ds(mult(i * 512 + at * HD, HD), HD) for i in range(NC)]
                gates = jnp.concatenate([wg[d, :] for d in deep], axis=0)
                ups = jnp.concatenate([wu[d, :] for d in deep], axis=0)
            if k:
                acc_ref[h, 0] += dot(xs[h, at], gates)
                acc_ref[h, 1] += dot(xs[h, at], ups)
            else:
                acc_ref[h, 0] = dot(xs[h, at], gates)
                acc_ref[h, 1] = dot(xs[h, at], ups)
        if k == 0:
            for side in range(2):
                for h in range(2):
                    x_line(h, side, side).wait_recv()
                    x_relay(h, side).start()
        if k == 1:
            pages_on(0)
            for copy in gt_copies(2):
                copy.wait_recv()
            for copy in gt_copies(3):
                copy.start()
            for kk in range(1, 4):
                st1(kk).wait_recv()
    squares = jnp.sum(st[...], axis=0)
    factor = lax.rsqrt(squares * (1.0 / D) + 1e-5)
    factor = jnp.broadcast_to(factor[0:1, :], (HD, TOK)).T
    for h in range(2):
        span = slice(h * HALF, (h + 1) * HALF)
        scale = factor[span, 0:1]
        gate = acc_ref[h, 0] * scale
        upward = acc_ref[h, 1] * scale
        hidden[span, :] = (gate / (1.0 + jnp.exp(-gate)) * upward).astype(BF)

    lane = lax.broadcasted_iota(jnp.int32, (HD, 1), 0)

    def roll_group(i, carry):
        fk = lane // 16
        r16 = lax.rem(lane, 16)
        column = lax.broadcasted_iota(jnp.int32, (HD, G_DEV * SPAN), 1)
        spans = jnp.zeros((32, G_DEV * SPAN), F32)
        for j in range(NC):
            from_c = lax.rem(c - j + NC, NC)
            token = (lax.rem(y - fk + 8, 4) * NC + from_c) * 4 + lax.rem(r16, 4)
            target = jnp.where((lane < 64) & (r16 < 12), (r16 // 4) * SPAN + token, -1)
            pick = jnp.where(column == target, 1.0, 0.0).astype(BF)
            spans = spans + dot(fs[i, j], pick)
        spans = spans.astype(BF)
        wide_column = lax.broadcasted_iota(jnp.int32, (SPAN, PAGE), 1)
        for g in range(G_DEV):
            at = lane + tb[i, PAGES + g : PAGES + g + 1, 0:1]
            spin = jnp.where(wide_column == lax.rem(at, PAGE), 1.0, 0.0).astype(BF)
            rolled[i * G_DEV + g] = dot(spans[:, g * SPAN : (g + 1) * SPAN], spin)
        return carry

    def pages_before():
        pages_on(1)
        for i in (1, 3):
            for copy in gt_copies(i):
                copy.wait_recv()
        lax.fori_loop(0, 4, roll_group, 0)

    def pages_in():
        pages_on(2)
        page = lax.broadcasted_iota(jnp.int32, (HD, 1), 0)
        gl = jnp.where(page >= NB, 1, 0) + jnp.where(page >= 2 * NB, 1, 0)
        b = page - gl * NB
        bb = jnp.minimum(b, 31)
        jj = lax.rem(c - bb + 32, NC)
        kk = lax.rem(y - bb // NC + 4, 4)
        slot = grp * PAGES + lax.broadcasted_iota(jnp.int32, (HD, HD), 1)
        where_ep = jnp.zeros((HD, HD), jnp.int32)
        where_left = jnp.full((HD, HD), -S_MAX, jnp.int32)
        where_roll = jnp.zeros((HD, HD), jnp.int32)
        for i in range(4):
            length = jnp.where(
                gl == 0,
                tb[i, PAGES : PAGES + 1, 0:1],
                jnp.where(gl == 1, tb[i, PAGES + 1 : PAGES + 2, 0:1], tb[i, PAGES + 2 : PAGES + 3, 0:1]),
            )
            match = (tb[i] == slot) & (page < PAGES)
            where_ep = jnp.where(match, ((i * G_DEV + gl) * NC + jj) * 4 + kk, where_ep)
            where_left = jnp.where(match, length - b * PAGE, where_left)
            where_roll = jnp.where(match, i * G_DEV + gl, where_roll)
        for n, table in enumerate((where_ep, where_left, where_roll)):
            plan[n] = jnp.broadcast_to(jnp.max(table, axis=0, keepdims=True), (8, HD))
        to_smem = pltpu.make_async_copy(plan, plan_smem, ep_loc.at[G_DEV])
        to_smem.start()
        for i in (1, 3):
            for g in range(G_DEV):
                g_copy(i, g).wait_recv()
        to_smem.wait()
        lanes = lax.broadcasted_iota(jnp.int32, (1, PAGE), 1)
        flat = ep.reshape(4 * G_DEV * NC * 4, 32, PAGE)

        def one_page(s, carry):
            left = plan_smem[1, 0, s]
            cached = flat[plan_smem[0, 0, s]].astype(F32)
            value = jnp.where(
                lanes < left,
                cached,
                jnp.where(lanes < left + SPAN, rolled[plan_smem[2, 0, s]], 0.0),
            )
            pool_ref[s] = value.astype(BF)
            return carry

        lax.fori_loop(0, PAGES, one_page, 0)

    weights[3].wait()
    finish_2 = scatter(1, hidden, wd, s2, q2, r2, t2, tr2, z2, zr2, pages_before, pages_in)
    for h in range(2):
        span = slice(h * HALF, (h + 1) * HALF)
        out_ref[span, :] = (hm[span, :].astype(F32) + fin[h]).astype(BF)

    for i in (1, 2, 3):
        for g in range(G_DEV):
            g_copy(i, g).wait_send()
        for copy in gt_copies(i):
            copy.wait_send()
    finish_1()
    finish_2()
    for h in range(2):
        x_flip(h).wait_send()
        for side in range(2):
            x_relay(h, side).wait_send()
            for part_ in range(2):
                x_line(h, side, part_).wait_send()
        for k in range(1, 4):
            for n in range(2):
                x_cross(h, k, n).wait_send()
    q_copy(1, 0).wait_send()
    for g in range(G_DEV):
        m_copy(g).wait_send()
    for k in range(1, 4):
        for n in range(2):
            q_copy(n, k).wait_send()
        for g in range(G_DEV):
            n_copy(g, k).wait_send()
        f_copy(k).wait_send()
        st1(k).wait_send()
        for g in range(G_DEV):
            kv_copy(k, g).wait_send()

    def sent(j):
        t_copy(j).wait_send()
        ss1(j).wait_send()
        for g in range(G_DEV):
            e_copy(g, j).wait_send()

    loop_c(sent)


def per_device(
    span_q, span_kv, kv_cache, resid, o_weight, norm_gain, w_gate, w_up, w_down, cached_len, page_table
):
    vmem = pl.BlockSpec(memory_space=pltpu.VMEM)
    anywhere = pl.BlockSpec(memory_space=pl.ANY)
    smem = pl.BlockSpec(memory_space=pltpu.SMEM)
    dma = pltpu.SemaphoreType.DMA
    scatter_bufs = [
        pltpu.VMEM((2, 4, HALF, 1024), BF), pltpu.VMEM((2, 2, HALF // 2, 1024), BF),
        pltpu.VMEM((2, 2, HALF, 1024), BF),
        pltpu.VMEM((2, 4, HALF, 2 * HD), BF), pltpu.VMEM((2, 4, HALF, 2 * HD), BF),
        pltpu.VMEM((2, HALF, HD), BF), pltpu.VMEM((2, HALF, HD), BF),
    ]
    table = jnp.concatenate([page_table, cached_len, jnp.zeros((HD - PAGES - G_DEV,), jnp.int32)])
    table = jnp.broadcast_to(table[:, None], (HD, HD))
    layer_out, decode_pool = pl.pallas_call(
        layer_kernel,
        out_shape=(
            jax.ShapeDtypeStruct((TOK, HD), BF),
            jax.ShapeDtypeStruct((PAGES, 32, PAGE), BF),
        ),
        in_specs=[
            vmem, vmem, anywhere, vmem, anywhere, vmem, anywhere, anywhere, anywhere, smem, vmem
        ],
        out_specs=(vmem, vmem),
        scratch_shapes=[
            pltpu.VMEM((HD, D), BF),
            pltpu.VMEM((D, FF_DEV), BF),
            pltpu.VMEM((D, FF_DEV), BF),
            pltpu.VMEM((FF_DEV, D), BF),
            pltpu.VMEM((4, G_DEV, 256, PAGE), BF),
            pltpu.VMEM((G_DEV, HD, SPAN), BF),
            pltpu.VMEM((G_DEV, HD, NC * SPAN), BF),
            pltpu.VMEM((16, 1024), BF),
            pltpu.VMEM((4, 16, 256), BF),
            pltpu.VMEM((256, HD), BF),
            pltpu.VMEM((G_DEV, 4, 2, HD + 16, SPAN), BF),
            pltpu.VMEM((G_DEV, 4, 2, HD + 16, SPAN), BF),
            pltpu.VMEM((G_DEV, HD + 16, SPAN), BF),
            pltpu.VMEM((G_DEV, HD + 16, SPAN), BF),
            pltpu.VMEM((TOK, HD), BF),
            *scatter_bufs,
            *scatter_bufs,
            pltpu.VMEM((2, 4, HALF, 1024), BF),
            pltpu.VMEM((TOK, HD), BF),
            pltpu.VMEM((NC, 8, TOK), F32),
            pltpu.VMEM((4, 8, TOK), F32),
            pltpu.VMEM((2, 2, HALF, FF_DEV), F32),
            pltpu.VMEM((TOK, FF_DEV), BF),
            pltpu.VMEM((2, HALF, 2 * HD), F32),
            pltpu.VMEM((2, HALF, HD), F32),
            pltpu.VMEM((4, G_DEV, NC, 4, 32, PAGE), BF),
            pltpu.VMEM((4, NC, 32, HD), BF),
            pltpu.VMEM((4, HD, HD), jnp.int32),
            pltpu.VMEM((4 * G_DEV, 32, PAGE), F32),
            pltpu.VMEM((3, 8, HD), jnp.int32),
            pltpu.SMEM((3, 8, HD), jnp.int32),
            dma((4,)), dma((G_DEV,)), dma((G_DEV + 1,)),
            dma((4, G_DEV)), dma((4, G_DEV)),
            dma((NC,)), dma((NC,)),
            dma((4,)), dma((4,)),
            dma((G_DEV, 4)), dma((G_DEV, 4)),
            dma((G_DEV,)), dma((G_DEV,)),
            dma((G_DEV, NC)), dma((G_DEV, NC)),
            dma((NC,)), dma((NC,)),
            dma((3, 2, 2, 2)), dma((3, 2, 2, 2)),
            dma((3, 2, 2)), dma((3, 2, 2)),
            dma((3, 2, 4, 2)), dma((3, 2, 4, 2)),
            dma((3, 2)), dma((3, 2)),
            dma((NC,)), dma((NC,)),
            dma((4,)), dma((4,)),
            dma((4, G_DEV)), dma((4, G_DEV)),
            dma((2, 4)), dma((2, 4)),
        ],
        compiler_params=pltpu.CompilerParams(
            collective_id=0, has_side_effects=True, vmem_limit_bytes=60 * 1024 * 1024
        ),
        name="layer",
    )(
        span_q, span_kv.transpose(0, 2, 1), kv_cache, resid, o_weight, norm_gain.reshape(1, HD),
        w_gate, w_up, w_down, cached_len, table,
    )
    return (layer_out, decode_pool)


def solution(mesh):
    in_specs = (
        P("grp", "dev"),
        P("grp", None, "dev"),
        P("grp", None, "dev"),
        P("grp", "dev"),
        P("dev", None),
        P("dev"),
        P(None, "dev"),
        P(None, "dev"),
        P("dev", None),
        P("grp"),
        P("grp"),
    )
    out_specs = (P("grp", "dev"), P("grp", "dev", None))
    return jax.shard_map(
        per_device, mesh=mesh, in_specs=in_specs, out_specs=out_specs, check_vma=False
    )
```

```python
import functools

import jax
import jax.numpy as jnp
from jax import lax
from jax.experimental import pallas as pl
from jax.experimental.pallas import tpu as pltpu
from jax.sharding import PartitionSpec as P

D = 4096
HD = 128
KVH = 4
PAGE = 256
G_DEV = 3
NB = 33
SPAN = 128
NY = 4
NC = 8
TOK = 384
HALF = 192
FF_DEV = 512
PAGES = 99
S_MAX = 8192
NEG = -1e30
SCALE = 1.4426950408889634 / HD**0.5
BF = jnp.bfloat16
F32 = jnp.float32
MESH = pl.DeviceIdType.MESH


def mult(value, by):
    return pl.multiple_of(value, by)


def dot(a, b, dims=(((1,), (0,)), ((), ()))):
    return lax.dot_general(a, b, dims, preferred_element_type=F32)


def layer_kernel(
    q_ref, skv_ref, kv_hbm, resid_ref, ow_hbm, gain_ref, wg_hbm, wu_hbm, wd_hbm, len_ref, table_ref,
    out_ref, pool_ref,
    ow, wg, wu, wd, kv, qt, qg, fr_src, fr, tr, ns, nr, ms, mr, att,
    s1, q1, r1, t1, tr1, z1, zr1, s2, q2, r2, t2, tr2, z2, zr2,
    xs, hm, ss, st, acc_ref, hidden, pair, fin, ep, fs, tb, rolled, plan, plan_smem,
    w_sem, kv_loc, ep_loc,
    kv_s, kv_r, q_s, q_r, f_s, f_r, n_s, n_r, m_s, m_r, e_s, e_r, t_s, t_r,
    p_s, p_r, l_s, l_r, c_s, c_r, z_s, z_r, ss_s, ss_r, st_s, st_r, g_s, g_r, gt_s, gt_r,
):
    grp = lax.axis_index("grp")
    me = lax.axis_index("dev")
    y = me // NC
    c = lax.rem(me, NC)
    x = lax.rem(me, 4)
    z = lax.rem(me // 4, 2)
    e = me // 4
    core = lax.rem(grp, 2)
    sibling = grp + 1 - 2 * core
    across = lax.rem(grp + 2, 4)

    def y_peer(k):
        return lax.rem(y + k, 4)

    def x_peer(k):
        return lax.rem(x + k, 4)

    def c_peer(j):
        return lax.rem(c + j, NC)

    def at_y(k):
        return y_peer(k) * NC + c

    def at_x(k):
        return e * 4 + x_peer(k)

    def at_c(j):
        return y * NC + c_peer(j)

    def remote(src, dst, send, recv, dev, group=None):
        return pltpu.make_async_remote_copy(
            src_ref=src, dst_ref=dst, send_sem=send, recv_sem=recv,
            device_id=(grp if group is None else group, dev), device_id_type=MESH)

    def loop_c(body):
        def step(j, carry):
            body(j)
            return carry

        lax.fori_loop(1, NC, step, 0)

    barrier = pltpu.get_barrier_semaphore()

    def greet(j):
        pl.semaphore_signal(barrier, inc=1, device_id=(grp, at_c(j)), device_id_type=MESH)

    loop_c(greet)
    for k in range(1, 4):
        pl.semaphore_signal(barrier, inc=1, device_id=(grp, at_y(k)), device_id_type=MESH)
    for other in (sibling, across):
        pl.semaphore_signal(barrier, inc=1, device_id=(other, me), device_id_type=MESH)

    own_kv = [
        pltpu.make_async_copy(
            kv_hbm.at[g, pl.ds(mult(y * 256, 256), 256)], kv.at[0, g], kv_loc.at[g]
        )
        for g in range(G_DEV)
    ]
    for copy in own_kv:
        copy.start()
    for g in range(G_DEV):
        qt[g] = q_ref[g * SPAN : (g + 1) * SPAN, :].astype(F32).T.astype(BF)
    fresh = jnp.zeros((16, 1024), F32)
    for g in range(G_DEV):
        row = lax.broadcasted_iota(jnp.int32, (16, 4), 0)
        col = lax.broadcasted_iota(jnp.int32, (16, 4), 1)
        pick = jnp.where(row == col + 4 * g, 1.0, 0.0).astype(BF)
        fresh = fresh + dot(pick, skv_ref[g])
    fr_src[...] = fresh.astype(BF)
    pl.semaphore_wait(barrier, NC - 1 + 3 + 2)
    at_flip = y * NC + lax.rem(c + 4, NC)

    def q_lanes(slot):
        return qg.at[:, :, pl.ds(slot * HD, HD)]

    def q_copy(n, k):
        src = q_lanes(4) if n and k else qt
        return remote(
            src, q_lanes(n * 4 + k), q_s.at[n * 4 + k], q_r.at[n * 4 + k],
            at_x(k) if k else at_flip)

    def f_copy(k):
        return remote(
            fr_src.at[:, pl.ds(mult(y_peer(k) * 256, 256), 256)],
            fr.at[k], f_s.at[k], f_r.at[k], at_y(k))

    def kv_copy(k, g):
        return remote(
            kv_hbm.at[g, pl.ds(mult(y_peer(k) * 256, 256), 256)],
            kv.at[k, g], kv_s.at[k, g], kv_r.at[k, g], at_y(k))

    q_copy(1, 0).start()
    for k in (1, 3, 2):
        q_copy(0, k).start()
    for k in range(1, 4):
        f_copy(k).start()
    for g in range(G_DEV):
        for k in (1, 3, 2):
            kv_copy(k, g).start()
    weights = [
        pltpu.make_async_copy(src, dst, w_sem.at[i])
        for i, (src, dst) in enumerate(((ow_hbm, ow), (wg_hbm, wg), (wu_hbm, wu), (wd_hbm, wd)))
    ]
    for copy in weights:
        copy.start()
    q_copy(1, 0).wait_recv()
    for k in (1, 3, 2):
        q_copy(1, k).start()
    tb[0] = table_ref[...]
    for g in range(G_DEV):
        qg[g, :, 0:HD] = qt[g]
    fr[0] = fr_src[:, pl.ds(mult(y * 256, 256), 256)]
    for k in range(1, 4):
        f_copy(k).wait_recv()
    fresh_rows = fr[...].reshape(64, 256)
    tr[...] = jnp.concatenate(
        [fresh_rows.astype(F32).T, jnp.zeros((256, 64), F32)], axis=1
    ).astype(BF)

    def t_copy(j):
        return remote(
            tr.at[pl.ds(mult(c_peer(j) * 32, 32), 32), :], fs.at[0, j], t_s.at[j], t_r.at[j], at_c(j))

    loop_c(lambda j: t_copy(j).start())
    fs[0, 0] = tr[pl.ds(mult(c * 32, 32), 32), :]
    for k in range(1, 4):
        for n in range(2):
            q_copy(n, k).wait_recv()

    rows = NC * SPAN
    top_dims = (((0,), (0,)), ((), ()))

    def n_copy(g, k):
        return remote(ns.at[g, k], nr.at[g, k], n_s.at[g, k], n_r.at[g, k], at_x(k))

    def m_copy(g):
        return remote(ms.at[g], mr.at[g], m_s.at[g], m_r.at[g], at_flip)

    def level_rows(level):
        hi = level.astype(BF).astype(F32)
        mid = (level - hi).astype(BF).astype(F32)
        low = level - hi - mid
        which = lax.broadcasted_iota(jnp.int32, (16, level.shape[1]), 0)
        return jnp.where(
            which == 0, hi, jnp.where(which == 1, mid, jnp.where(which == 2, low, 0.0))
        )

    def merge(parts):
        levels = [jnp.sum(p[HD : HD + 16, :].astype(F32), axis=0, keepdims=True) for p in parts]
        top = functools.reduce(jnp.maximum, levels)
        scales = [jnp.exp2(level - top) for level in levels]
        total = sum(scales)
        summed = sum(p[0:HD, :].astype(F32) * scale for p, scale in zip(parts, scales))
        return summed / total, top + jnp.log2(total)

    def merge_other(g):
        for k in range(1, 4):
            n_copy(g, k).wait_recv()
        value, level = merge([nr[g, k, 1] for k in range(4)])
        ms[g, 0:HD, :] = value.astype(BF)
        ms[g, HD : HD + 16, :] = level_rows(level).astype(BF)
        m_copy(g).start()

    def e_copy(g, j):
        return remote(
            kv.at[:, g, pl.ds(mult(c_peer(j) * 32, 32), 32), :],
            ep.at[0, g, j], e_s.at[g, j], e_r.at[g, j], at_c(j))

    own_pages = [
        pltpu.make_async_copy(
            kv.at[:, g, pl.ds(mult(c * 32, 32), 32), :], ep.at[0, g, 0], ep_loc.at[g]
        )
        for g in range(G_DEV)
    ]

    for g in range(G_DEV):
        length = len_ref[g]
        high = jnp.full((1, rows), -1e20, F32)
        total = jnp.zeros((1, rows), F32)
        acc = jnp.zeros((HD, rows), F32)

        def block(score, value, high, total, acc):
            new = jnp.maximum(high, jnp.max(score, axis=0, keepdims=True))
            keep = jnp.exp2((high - new) * SCALE)
            weight = jnp.exp2((score - new) * SCALE)
            total = total * keep + jnp.sum(weight, axis=0, keepdims=True)
            acc = acc * keep + dot(value, weight.astype(BF))
            return new, total, acc

        r = lax.broadcasted_iota(jnp.int32, (64, rows), 0)
        token = lax.rem(lax.broadcasted_iota(jnp.int32, (64, rows), 1), SPAN)
        src_y = lax.rem(y - r // 16 + 4, 4)
        r16 = lax.rem(r, 16)
        fresh_at = (src_y * NC + c) * 4 + lax.rem(r16, 4)
        ok = (r16 // 4 == g) & (fresh_at <= token)
        score = dot(fresh_rows[:, 0:HD], qg[g])
        score = jnp.where(ok, score, NEG)
        high, total, acc = block(score, tr[HD : 2 * HD, 0:64], high, total, acc)
        own_kv[g].wait()
        if g < G_DEV - 1:
            for k in range(1, 4):
                kv_copy(k, g).wait_recv()
            loop_c(lambda j, g=g: e_copy(g, j).start())
        for k in (0, 1, 3, 2):
            if k and g == G_DEV - 1:
                kv_copy(k, g).wait_recv()
            first = (lax.rem(y - k + 4, 4) * NC + c) * PAGE
            at = first + lax.broadcasted_iota(jnp.int32, (PAGE, 1), 0)
            score = dot(kv[k, g, 0:HD, :], qg[g], top_dims)
            score = jnp.where(at < length, score, NEG)
            high, total, acc = block(score, kv[k, g, HD : 2 * HD, :], high, total, acc)
        some = total > 0.0
        scaled = acc * jnp.where(some, 1.0 / jnp.where(some, total, 1.0), 0.0)
        level = jnp.where(some, high * SCALE + jnp.log2(jnp.where(some, total, 1.0)), NEG)
        rest = level_rows(level)
        for n in range(2):
            for k in range(4):
                lanes = slice((n * 4 + k) * HD, (n * 4 + k + 1) * HD)
                buf = ns if k else nr
                buf[g, (4 - k) % 4, n, 0:HD, :] = scaled[:, lanes].astype(BF)
                buf[g, (4 - k) % 4, n, HD : HD + 16, :] = rest[:, lanes].astype(BF)
        for k in (1, 3, 2):
            n_copy(g, k).start()
        own_pages[g].start()
        if g:
            merge_other(g - 1)

    merge_other(G_DEV - 1)
    loop_c(lambda j: e_copy(G_DEV - 1, j).start())
    for g in range(G_DEV):
        m_copy(g).wait_recv()
        value, _ = merge([nr[g, k, 0] for k in range(4)] + [mr[g]])
        att[g * SPAN : (g + 1) * SPAN, :] = value.T.astype(BF)

    def g_copy(i, g):
        target = across if i == 2 else sibling
        from_slot = 2 if i == 3 else 0
        return remote(ep.at[from_slot, g], ep.at[i, g], g_s.at[i, g], g_r.at[i, g], me, target)

    def gt_copies(i):
        target = across if i == 2 else sibling
        from_slot = 2 if i == 3 else 0
        return (
            remote(fs.at[from_slot], fs.at[i], gt_s.at[0, i], gt_r.at[0, i], me, target),
            remote(tb.at[from_slot], tb.at[i], gt_s.at[1, i], gt_r.at[1, i], me, target),
        )

    def pages_out(g):
        loop_c(lambda j: e_copy(g, j).wait_recv())
        own_pages[g].wait()
        g_copy(2, g).start()
        g_copy(1, g).start()

    def pages_on(g):
        g_copy(2, g).wait_recv()
        g_copy(3, g).start()

    quarter = HALF // 2
    second_at = (c, e)
    flip_at = (lax.rem(c + 4, NC), e + 1 - 2 * z)

    def line(h, k):
        return at_x(k) if h else at_y(k)

    def cross(h, k):
        return at_y(k) if h else at_x(k)

    def strip(part):
        return pl.ds(part * quarter, quarter)

    def scatter(turn, lhs, w, s, q, r, t, tr_, zt, zr, middle, later):
        def relay(h, side):
            return remote(
                s.at[h, 2, strip(side)], q.at[h, side],
                l_s.at[turn, h, side], l_r.at[turn, h, side], line(h, 1 + 2 * side))

        def first(h, side, part):
            return remote(
                s.at[h, 1 + 2 * side, strip(part)], r.at[h, side, strip(part)],
                p_s.at[turn, h, side, part], p_r.at[turn, h, side, part], line(h, 1 + 2 * side))

        def second(h, k):
            return remote(
                t.at[h, k], tr_.at[h, k], c_s.at[turn, h, k, 0], c_r.at[turn, h, k, 0], cross(h, k))

        def third(h):
            return remote(zt.at[h], zr.at[h], z_s.at[turn, h], z_r.at[turn, h], at_flip)

        def part(h, k):
            left = lhs[h * HALF : (h + 1) * HALF, :]
            if h == 0:
                cols = w[:, pl.ds(mult(y_peer(k) * 1024, 1024), 1024)]
            else:
                cols = jnp.concatenate(
                    [w[:, pl.ds(mult(i * 512 + x_peer(k) * HD, HD), HD)] for i in range(NC)], axis=1
                )
            s[h, k] = dot(left, cols).astype(BF)

        for h in range(2):
            part(h, 2)
            for side in range(2):
                relay(h, side).start()
        for side in range(2):
            for h in range(2):
                part(h, 1 + 2 * side)
                first(h, side, 1 - side).start()
        for side in range(2):
            for h in range(2):
                relay(h, side).wait_recv()
                rows_ = strip(side)
                both = s[h, 1 + 2 * side, rows_].astype(F32) + q[h, side].astype(F32)
                s[h, 1 + 2 * side, rows_] = both.astype(BF)
                first(h, side, side).start()
        for h in range(2):
            part(h, 0)
        middle()

        def summed(h, k):
            if h == 0:
                at = x_peer(k) * HD
                views = [pl.ds(mult(at, HD), HD), pl.ds(mult(at + 512, HD), HD)]
            else:
                views = [pl.ds(mult(y_peer(k) * 256, 256), 256)]
            blocks = [
                s[h, 0, :, v].astype(F32) + r[h, 0, :, v].astype(F32) + r[h, 1, :, v].astype(F32)
                for v in views
            ]
            return blocks[0] if h else jnp.concatenate(blocks, axis=1)

        for h in range(2):
            for side in range(2):
                for part_ in range(2):
                    first(h, side, part_).wait_recv()
            for k in (1, 3, 2):
                t[h, k] = summed(h, k).astype(BF)
                second(h, k).start()
        later()
        mine, other = pl.ds(mult(z * HD, HD), HD), pl.ds(mult((1 - z) * HD, HD), HD)
        for h in range(2):
            pair[h] = summed(h, 0)
        for h in range(2):
            for k in (1, 3, 2):
                second(h, k).wait_recv()
            total = pair[h]
            for k in range(1, 4):
                total = total + tr_[h, k].astype(F32)
            pair[h] = total
            zt[h] = pair[h, :, other].astype(BF)
            third(h).start()
        for h in range(2):
            third(h).wait_recv()
            fin[h] = pair[h, :, mine] + zr[h].astype(F32)

        def finish():
            for h in range(2):
                third(h).wait_send()
                for side in range(2):
                    relay(h, side).wait_send()
                    for part_ in range(2):
                        first(h, side, part_).wait_send()
                for k in range(1, 4):
                    second(h, k).wait_send()

        return finish

    weights[0].wait()

    def middle_1():
        loop_c(lambda j: t_copy(j).wait_recv())
        for copy in gt_copies(2) + gt_copies(1):
            copy.start()
        pages_out(0)

    finish_1 = scatter(0, att, ow, s1, q1, r1, t1, tr1, z1, zr1, middle_1, lambda: None)

    ones = jnp.ones((8, HD), F32)
    for h in range(2):
        span = slice(h * HALF, (h + 1) * HALF)
        mid_bf = (resid_ref[span, :].astype(F32) + fin[h]).astype(BF)
        hm[span, :] = mid_bf
        wide = mid_bf.astype(F32)
        xs[h, x if h else y, :, pl.ds(mult(second_at[h] * HD, HD), HD)] = (
            wide * gain_ref[...]
        ).astype(BF)

    prime = (y, x)

    def x_flip(h):
        view = xs.at[h, prime[h], :, pl.ds(mult(second_at[h] * HD, HD), HD)]
        return remote(view, view, z_s.at[2, h], z_r.at[2, h], at_flip)

    def x_cross(h, k, n):
        at = flip_at[h] if n else second_at[h]
        view = xs.at[h, prime[h], :, pl.ds(mult(at * HD, HD), HD)]
        return remote(view, view, c_s.at[2, h, k, n], c_r.at[2, h, k, n], cross(h, k))

    def x_line(h, side, part):
        view = xs.at[h, prime[h], strip(part)]
        return remote(
            view, view, p_s.at[2, h, side, part], p_r.at[2, h, side, part], line(h, 1 + 2 * side))

    def x_relay(h, side):
        view = xs.at[h, lax.rem(prime[h] + 3 - 2 * side, 4), strip(side)]
        return remote(
            view, view, l_s.at[2, h, side], l_r.at[2, h, side], line(h, 1 + 2 * side))

    def ss1(j):
        return remote(ss.at[0], ss.at[j], ss_s.at[j], ss_r.at[j], at_c(j))

    def st1(k):
        return remote(st.at[0], st.at[k], st_s.at[k], st_r.at[k], at_y(k))

    for h in range(2):
        x_flip(h).start()
        for k in (1, 3, 2):
            x_cross(h, k, 0).start()
    wide = hm[...].astype(F32)
    ss[0] = lax.dot_general(
        ones, wide * wide, (((1,), (1,)), ((), ())),
        precision=lax.Precision.HIGHEST, preferred_element_type=F32)
    loop_c(lambda j: ss1(j).start())
    for h in range(2):
        x_flip(h).wait_recv()
        for k in (1, 3, 2):
            x_cross(h, k, 1).start()
    pages_out(1)
    for h in range(2):
        for n in range(2):
            for k in range(1, 4):
                x_cross(h, k, n).wait_recv()
        for n in range(2):
            for side in range(2):
                x_line(h, side, (side + n) % 2).start()
    pages_out(2)
    loop_c(lambda j: ss1(j).wait_recv())
    st[0] = jnp.sum(ss[...], axis=0)
    for k in range(1, 4):
        st1(k).start()

    weights[1].wait()
    weights[2].wait()
    for k in (0, 1, 3, 2):
        for h in range(2):
            if k == 2:
                x_relay(h, 0).wait_recv()
                x_relay(h, 1).wait_recv()
            elif k:
                x_line(h, k // 2, 1 - k // 2).wait_recv()
            if h == 0:
                at = lax.rem(y - k + 4, 4)
                deep = pl.ds(mult(at * 1024, 1024), 1024)
                gates, ups = wg[deep, :], wu[deep, :]
            else:
                at = lax.rem(x - k + 4, 4)
                deep = [pl.ds(mult(i * 512 + at * HD, HD), HD) for i in range(NC)]
                gates = jnp.concatenate([wg[d, :] for d in deep], axis=0)
                ups = jnp.concatenate([wu[d, :] for d in deep], axis=0)
            if k:
                acc_ref[h, 0] += dot(xs[h, at], gates)
                acc_ref[h, 1] += dot(xs[h, at], ups)
            else:
                acc_ref[h, 0] = dot(xs[h, at], gates)
                acc_ref[h, 1] = dot(xs[h, at], ups)
        if k == 0:
            for side in range(2):
                for h in range(2):
                    x_line(h, side, side).wait_recv()
                    x_relay(h, side).start()
        if k == 1:
            pages_on(0)
            for copy in gt_copies(2):
                copy.wait_recv()
            for copy in gt_copies(3):
                copy.start()
            for kk in range(1, 4):
                st1(kk).wait_recv()
    squares = jnp.sum(st[...], axis=0)
    factor = lax.rsqrt(squares * (1.0 / D) + 1e-5)
    factor = jnp.broadcast_to(factor[0:1, :], (HD, TOK)).T
    for h in range(2):
        span = slice(h * HALF, (h + 1) * HALF)
        scale = factor[span, 0:1]
        gate = acc_ref[h, 0] * scale
        upward = acc_ref[h, 1] * scale
        hidden[span, :] = (gate / (1.0 + jnp.exp(-gate)) * upward).astype(BF)

    lane = lax.broadcasted_iota(jnp.int32, (HD, 1), 0)

    def roll_group(i, carry):
        fk = lane // 16
        r16 = lax.rem(lane, 16)
        column = lax.broadcasted_iota(jnp.int32, (HD, G_DEV * SPAN), 1)
        spans = jnp.zeros((32, G_DEV * SPAN), F32)
        for j in range(NC):
            from_c = lax.rem(c - j + NC, NC)
            token = (lax.rem(y - fk + 8, 4) * NC + from_c) * 4 + lax.rem(r16, 4)
            target = jnp.where((lane < 64) & (r16 < 12), (r16 // 4) * SPAN + token, -1)
            pick = jnp.where(column == target, 1.0, 0.0).astype(BF)
            spans = spans + dot(fs[i, j], pick)
        spans = spans.astype(BF)
        wide_column = lax.broadcasted_iota(jnp.int32, (SPAN, PAGE), 1)
        for g in range(G_DEV):
            at = lane + tb[i, PAGES + g : PAGES + g + 1, 0:1]
            spin = jnp.where(wide_column == lax.rem(at, PAGE), 1.0, 0.0).astype(BF)
            rolled[i * G_DEV + g] = dot(spans[:, g * SPAN : (g + 1) * SPAN], spin)
        return carry

    def pages_before():
        pages_on(1)
        for i in (1, 3):
            for copy in gt_copies(i):
                copy.wait_recv()
        lax.fori_loop(0, 4, roll_group, 0)

    def pages_in():
        pages_on(2)
        page = lax.broadcasted_iota(jnp.int32, (HD, 1), 0)
        gl = jnp.where(page >= NB, 1, 0) + jnp.where(page >= 2 * NB, 1, 0)
        b = page - gl * NB
        bb = jnp.minimum(b, 31)
        jj = lax.rem(c - bb + 32, NC)
        kk = lax.rem(y - bb // NC + 4, 4)
        slot = grp * PAGES + lax.broadcasted_iota(jnp.int32, (HD, HD), 1)
        where_ep = jnp.zeros((HD, HD), jnp.int32)
        where_left = jnp.full((HD, HD), -S_MAX, jnp.int32)
        where_roll = jnp.zeros((HD, HD), jnp.int32)
        for i in range(4):
            length = jnp.where(
                gl == 0,
                tb[i, PAGES : PAGES + 1, 0:1],
                jnp.where(gl == 1, tb[i, PAGES + 1 : PAGES + 2, 0:1], tb[i, PAGES + 2 : PAGES + 3, 0:1]),
            )
            match = (tb[i] == slot) & (page < PAGES)
            where_ep = jnp.where(match, ((i * G_DEV + gl) * NC + jj) * 4 + kk, where_ep)
            where_left = jnp.where(match, length - b * PAGE, where_left)
            where_roll = jnp.where(match, i * G_DEV + gl, where_roll)
        for n, table in enumerate((where_ep, where_left, where_roll)):
            plan[n] = jnp.broadcast_to(jnp.max(table, axis=0, keepdims=True), (8, HD))
        to_smem = pltpu.make_async_copy(plan, plan_smem, ep_loc.at[G_DEV])
        to_smem.start()
        for i in (1, 3):
            for g in range(G_DEV):
                g_copy(i, g).wait_recv()
        to_smem.wait()
        lanes = lax.broadcasted_iota(jnp.int32, (1, PAGE), 1)
        flat = ep.reshape(4 * G_DEV * NC * 4, 32, PAGE)

        def one_page(s, carry):
            left = plan_smem[1, 0, s]
            cached = flat[plan_smem[0, 0, s]].astype(F32)
            value = jnp.where(
                lanes < left,
                cached,
                jnp.where(lanes < left + SPAN, rolled[plan_smem[2, 0, s]], 0.0),
            )
            pool_ref[s] = value.astype(BF)
            return carry

        lax.fori_loop(0, PAGES, one_page, 0)

    weights[3].wait()
    finish_2 = scatter(1, hidden, wd, s2, q2, r2, t2, tr2, z2, zr2, pages_before, pages_in)
    for h in range(2):
        span = slice(h * HALF, (h + 1) * HALF)
        out_ref[span, :] = (hm[span, :].astype(F32) + fin[h]).astype(BF)

    for i in (1, 2, 3):
        for g in range(G_DEV):
            g_copy(i, g).wait_send()
        for copy in gt_copies(i):
            copy.wait_send()
    finish_1()
    finish_2()
    for h in range(2):
        x_flip(h).wait_send()
        for side in range(2):
            x_relay(h, side).wait_send()
            for part_ in range(2):
                x_line(h, side, part_).wait_send()
        for k in range(1, 4):
            for n in range(2):
                x_cross(h, k, n).wait_send()
    q_copy(1, 0).wait_send()
    for g in range(G_DEV):
        m_copy(g).wait_send()
    for k in range(1, 4):
        for n in range(2):
            q_copy(n, k).wait_send()
        for g in range(G_DEV):
            n_copy(g, k).wait_send()
        f_copy(k).wait_send()
        st1(k).wait_send()
        for g in range(G_DEV):
            kv_copy(k, g).wait_send()

    def sent(j):
        t_copy(j).wait_send()
        ss1(j).wait_send()
        for g in range(G_DEV):
            e_copy(g, j).wait_send()

    loop_c(sent)


def per_device(
    span_q, span_kv, kv_cache, resid, o_weight, norm_gain, w_gate, w_up, w_down, cached_len, page_table
):
    vmem = pl.BlockSpec(memory_space=pltpu.VMEM)
    anywhere = pl.BlockSpec(memory_space=pl.ANY)
    smem = pl.BlockSpec(memory_space=pltpu.SMEM)
    dma = pltpu.SemaphoreType.DMA
    scatter_bufs = [
        pltpu.VMEM((2, 4, HALF, 1024), BF), pltpu.VMEM((2, 2, HALF // 2, 1024), BF),
        pltpu.VMEM((2, 2, HALF, 1024), BF),
        pltpu.VMEM((2, 4, HALF, 2 * HD), BF), pltpu.VMEM((2, 4, HALF, 2 * HD), BF),
        pltpu.VMEM((2, HALF, HD), BF), pltpu.VMEM((2, HALF, HD), BF),
    ]
    table = jnp.concatenate([page_table, cached_len, jnp.zeros((HD - PAGES - G_DEV,), jnp.int32)])
    table = jnp.broadcast_to(table[:, None], (HD, HD))
    layer_out, decode_pool = pl.pallas_call(
        layer_kernel,
        out_shape=(
            jax.ShapeDtypeStruct((TOK, HD), BF),
            jax.ShapeDtypeStruct((PAGES, 32, PAGE), BF),
        ),
        in_specs=[
            vmem, vmem, anywhere, vmem, anywhere, vmem, anywhere, anywhere, anywhere, smem, vmem
        ],
        out_specs=(vmem, vmem),
        scratch_shapes=[
            pltpu.VMEM((HD, D), BF),
            pltpu.VMEM((D, FF_DEV), BF),
            pltpu.VMEM((D, FF_DEV), BF),
            pltpu.VMEM((FF_DEV, D), BF),
            pltpu.VMEM((4, G_DEV, 256, PAGE), BF),
            pltpu.VMEM((G_DEV, HD, SPAN), BF),
            pltpu.VMEM((G_DEV, HD, NC * SPAN), BF),
            pltpu.VMEM((16, 1024), BF),
            pltpu.VMEM((4, 16, 256), BF),
            pltpu.VMEM((256, HD), BF),
            pltpu.VMEM((G_DEV, 4, 2, HD + 16, SPAN), BF),
            pltpu.VMEM((G_DEV, 4, 2, HD + 16, SPAN), BF),
            pltpu.VMEM((G_DEV, HD + 16, SPAN), BF),
            pltpu.VMEM((G_DEV, HD + 16, SPAN), BF),
            pltpu.VMEM((TOK, HD), BF),
            *scatter_bufs,
            *scatter_bufs,
            pltpu.VMEM((2, 4, HALF, 1024), BF),
            pltpu.VMEM((TOK, HD), BF),
            pltpu.VMEM((NC, 8, TOK), F32),
            pltpu.VMEM((4, 8, TOK), F32),
            pltpu.VMEM((2, 2, HALF, FF_DEV), F32),
            pltpu.VMEM((TOK, FF_DEV), BF),
            pltpu.VMEM((2, HALF, 2 * HD), F32),
            pltpu.VMEM((2, HALF, HD), F32),
            pltpu.VMEM((4, G_DEV, NC, 4, 32, PAGE), BF),
            pltpu.VMEM((4, NC, 32, HD), BF),
            pltpu.VMEM((4, HD, HD), jnp.int32),
            pltpu.VMEM((4 * G_DEV, 32, PAGE), F32),
            pltpu.VMEM((3, 8, HD), jnp.int32),
            pltpu.SMEM((3, 8, HD), jnp.int32),
            dma((4,)), dma((G_DEV,)), dma((G_DEV + 1,)),
            dma((4, G_DEV)), dma((4, G_DEV)),
            dma((NC,)), dma((NC,)),
            dma((4,)), dma((4,)),
            dma((G_DEV, 4)), dma((G_DEV, 4)),
            dma((G_DEV,)), dma((G_DEV,)),
            dma((G_DEV, NC)), dma((G_DEV, NC)),
            dma((NC,)), dma((NC,)),
            dma((3, 2, 2, 2)), dma((3, 2, 2, 2)),
            dma((3, 2, 2)), dma((3, 2, 2)),
            dma((3, 2, 4, 2)), dma((3, 2, 4, 2)),
            dma((3, 2)), dma((3, 2)),
            dma((NC,)), dma((NC,)),
            dma((4,)), dma((4,)),
            dma((4, G_DEV)), dma((4, G_DEV)),
            dma((2, 4)), dma((2, 4)),
        ],
        compiler_params=pltpu.CompilerParams(
            collective_id=0, has_side_effects=True, vmem_limit_bytes=60 * 1024 * 1024
        ),
        name="layer",
    )(
        span_q, span_kv.transpose(0, 2, 1), kv_cache, resid, o_weight, norm_gain.reshape(1, HD),
        w_gate, w_up, w_down, cached_len, table,
    )
    return (layer_out, decode_pool)


def solution(mesh):
    in_specs = (
        P("grp", "dev"),
        P("grp", None, "dev"),
        P("grp", None, "dev"),
        P("grp", "dev"),
        P("dev", None),
        P("dev"),
        P(None, "dev"),
        P(None, "dev"),
        P("dev", None),
        P("grp"),
        P("grp"),
    )
    out_specs = (P("grp", "dev"), P("grp", "dev", None))
    return jax.shard_map(
        per_device, mesh=mesh, in_specs=in_specs, out_specs=out_specs, check_vma=False
    )
```
